256 devices in a mesh: row: 16 (over y, x_hi, core), col: 16 (over x_lo, z).
Axes of the slice: x: 4 (x_hi: 2, x_lo: 2; x = x_hi * 2 + x_lo), y: 4, z: 8, core: 2. Of those that a mesh axis runs over, the one named last changes fastest.
Arguments:
- start_block: float32 [32768, 128], P('row'), may hold values from -400 to 400
- tiles: bfloat16 [16, 16, 16, 12, 128, 128], P('row', 'col'), may hold values from -0.02734375 to 0.02734375
- band_offsets: int32 [16, 16, 12], P('row', 'col'), may hold values from 0 to 15, as said below
Outputs:
- lanczos_alpha: float32 [2, 128], replicated
- lanczos_beta: float32 [2, 128], replicated
- next_vector: float32 [32768, 128], P('row')
The draws below stay inside these ranges and needn't reach their ends.
Inputs may be any that keep to these rules, and one draw needn't show every extreme that they name: `band_offsets`: on each device the 12 offsets are distinct, the first is 0 and the second is 15.
All inputs are finite; a program needn't handle non-finite values.
Results may differ from the reference program's by a relative error of at most 0.0057.
Values may be sent and summed in bfloat16 or wider, within the bound.
No kernel may reach another device: no remote copies, remote signals or barrier semaphores. Data moves between devices by JAX's collectives and lax.ppermute only.
A program may use at most 128 MiB of HBM per device.

```python
import math
import jax
import jax.numpy as jnp
from jax import lax

TILE = 128
TB = 16
NPR = 12
NV = 128
ROWS = 32768
N_ROW = 16
N_COL = 16


def draw_band_offsets(key, part):
    key = jax.random.fold_in(key, 11)
    keys = jax.random.split(key, N_ROW * N_COL)

    def single(small_key):
        head = jnp.zeros((1,), jnp.int32)
        others = jax.random.permutation(small_key, TB - 2)[:NPR - 2].astype(jnp.int32) + 1
        top = jnp.full((1,), TB - 1, jnp.int32)
        return jnp.concatenate([head, top, others])
    return jax.vmap(single)(keys).reshape(N_ROW, N_COL, NPR)


def draw_start_block(key, part):
    key = jax.random.fold_in(key, 5)
    key_base, key_rows, key_cols = jax.random.split(key, 3)
    row_scale = jnp.exp(jax.random.uniform(key_rows, (ROWS, 1), jnp.float32, 0.0, math.log(10.0)))
    col_scale = jnp.exp(jax.random.uniform(key_cols, (1, NV), jnp.float32, 0.0, math.log(10.0)))
    base = jax.random.truncated_normal(key_base, -4.0, 4.0, (ROWS, NV), jnp.float32)
    return (base * row_scale * col_scale).astype(jnp.float32)


def level_of(rng, extent, cuts, least, high):
    level, own = 1.0, jax.random.fold_in(rng, 6)
    for dim, blocks in cuts:
        steps = jnp.exp(jax.random.uniform(jax.random.fold_in(own, dim), (blocks,), jnp.float32, least / len(cuts), high / len(cuts)))
        level = level * jnp.repeat(steps, extent[dim] // blocks).reshape([-1 if axis == dim else 1 for axis in range(len(extent))])
    return level


def scatter_about(own_key, extent, scale, limit, cuts=(), kind=jnp.bfloat16):
    factor_of = level_of(own_key, extent, cuts, -0.22, 0.18) if cuts else 1.0
    result = jax.random.normal(own_key, extent, jnp.float32) * scale * factor_of
    return jnp.minimum(jnp.maximum(result, -limit), limit).astype(kind)


def setup_inputs(seed: int = 0) -> dict:
    seeds = jax.random.split(jax.random.key(seed), 4)
    return {
        "start_block": draw_start_block(jax.random.fold_in(seeds[3], 71), 0),
        "tiles": scatter_about(seeds[1], (N_ROW, N_COL, TB, NPR, TILE, TILE), (2 * N_COL * NPR * TILE) ** -0.5, 0.02734375, ((0, 16), (1, 16))),
        "band_offsets": draw_band_offsets(jax.random.fold_in(seeds[3], 71), 0),
    }


EPS = 1e-06

def block_terms(tiles_dev, offsets, near, far):
    column_index = (jnp.arange(TB, dtype=jnp.int32)[:, None] + offsets[None, :].astype(jnp.int32)) % TB
    forward = jnp.einsum('bkij,bkjv->biv', tiles_dev.astype(jnp.float32), far[column_index].astype(jnp.float32), precision=lax.Precision.HIGHEST)
    backward = jnp.einsum('bkji,bjv->bkiv', tiles_dev.astype(jnp.float32), near.astype(jnp.float32), precision=lax.Precision.HIGHEST)
    placed = (column_index[None, :, :] == jnp.arange(TB, dtype=jnp.int32)[:, None, None]).astype(jnp.float32)
    moved = jnp.einsum('sbk,bkiv->siv', placed, backward, precision=lax.Precision.HIGHEST)
    return (forward, moved.astype(jnp.bfloat16))

def apply_h(vector, tiles, band_offsets):
    blocks = vector.astype(jnp.bfloat16).reshape(N_ROW, TB, TILE, NV)

    def step(index, total):
        index = jnp.asarray(index).astype(jnp.int32)
        r = index // N_COL
        c = index % N_COL
        s = (r + c) % N_ROW
        forward, moved = block_terms(tiles[r, c], band_offsets[r, c], blocks[r], blocks[s])
        total = total.at[r].add(forward)
        total = total.at[s].add(moved.astype(jnp.float32))
        return total
    total = lax.fori_loop(0, N_ROW * N_COL, step, jnp.zeros((N_ROW, TB, TILE, NV), jnp.float32))
    return total.reshape(N_ROW * TB * TILE, NV)

def coefficients(q, w):
    alpha = lax.optimization_barrier(jnp.mean(q * w, axis=0))
    w = w - alpha * q
    beta = jnp.sqrt(lax.optimization_barrier(jnp.mean(w * w, axis=0)) + EPS)
    return (alpha, beta, w / beta)

def reference(start_block, tiles, band_offsets):
    q_first = start_block / jnp.sqrt(lax.optimization_barrier(jnp.mean(start_block * start_block, axis=0)) + EPS)
    w = apply_h(q_first, tiles, band_offsets)
    alpha_one, beta_one, q_second = coefficients(q_first, w)
    w = apply_h(q_second, tiles, band_offsets) - beta_one * q_first
    alpha_two, beta_two, q_third = coefficients(q_second, w)
    return (jnp.stack([alpha_one, alpha_two]), jnp.stack([beta_one, beta_two]), q_third)
```

```python
import functools

import jax
import jax.numpy as jnp
from jax import lax
from jax.experimental import pallas as pl
from jax.experimental.pallas import tpu as pltpu
from jax.sharding import PartitionSpec as P

EPS = 1e-06
TINY = 1e-30
WIRE = jnp.float16
PRODUCT_SCALE = 128.0
SEGMENT_SCALE = 1024.0
ROWS_PER_STEP = 2


def split_halves(value):
    high = value.astype(jnp.bfloat16)
    low = (value - high.astype(jnp.float32)).astype(jnp.bfloat16)
    return jnp.concatenate([high, low], axis=1)


def forward_kernel(offsets, tiles, far, out, halves):
    step = pl.program_id(0)
    blocks, width, columns = far.shape

    @pl.when(step == 0)
    def _():
        for block in range(blocks):
            halves[block] = split_halves(far[block])

    kept = tiles.shape[1]
    for local in range(tiles.shape[0]):
        row = step * tiles.shape[0] + local
        total = jnp.zeros((width, 2 * columns), jnp.float32)
        for k in range(0, kept, 2):
            first = halves[lax.rem(row + offsets[k], blocks)]
            second = halves[lax.rem(row + offsets[k + 1], blocks)]
            left = jnp.concatenate([tiles[local, k], tiles[local, k + 1]], axis=1)
            right = jnp.concatenate([first, second], axis=0)
            total += jnp.dot(left, right, preferred_element_type=jnp.float32)
        out[local] = total[:, :columns] + total[:, columns:]


def backward_kernel(exact, offsets, tiles, near, out, squares, total):
    step = pl.program_id(0)
    blocks, columns, width = total.shape
    kept = tiles.shape[1]

    @pl.when(step == 0)
    def _():
        total[...] = jnp.zeros_like(total)
        squares[...] = jnp.zeros_like(squares)

    for local in range(tiles.shape[0]):
        row = step * tiles.shape[0] + local
        value = near[local]
        squares[...] += jnp.sum(value * value, axis=0, keepdims=True)
        turned = value.T
        high = turned.astype(jnp.bfloat16)
        if exact:
            low = (turned - high.astype(jnp.float32)).astype(jnp.bfloat16)
            left = jnp.concatenate([high, low], axis=0)
        else:
            left = high
        for k in range(0, kept, 2):
            right = jnp.concatenate([tiles[local, k], tiles[local, k + 1]], axis=1)
            part = jnp.dot(left, right, preferred_element_type=jnp.float32)
            if exact:
                part = part[:columns] + part[columns:]
            total[lax.rem(row + offsets[k], blocks)] += part[:, :width]
            total[lax.rem(row + offsets[k + 1], blocks)] += part[:, width:]

    @pl.when(step == pl.num_programs(0) - 1)
    def _():
        rows = blocks * width
        scale = SEGMENT_SCALE * lax.rsqrt(squares[...] * (1.0 / rows) + TINY)
        for block in range(blocks):
            out[block] = total[block].T * scale


def cost(tiles, passes):
    blocks, kept, width, _ = tiles.shape
    flops = 2 * passes * blocks * kept * width**3
    return pl.CostEstimate(flops=flops, bytes_accessed=2 * tiles.size, transcendentals=0)


def forward_product(tiles, offsets, far):
    blocks, kept, width, _ = tiles.shape
    columns = far.shape[-1]
    per = ROWS_PER_STEP
    return pl.pallas_call(
        forward_kernel,
        out_shape=jax.ShapeDtypeStruct((blocks, width, columns), jnp.float32),
        grid_spec=pltpu.PrefetchScalarGridSpec(
            num_scalar_prefetch=1,
            grid=(blocks // per,),
            in_specs=[
                pl.BlockSpec((per, kept, width, width), lambda i, o: (i, 0, 0, 0)),
                pl.BlockSpec((blocks, width, columns), lambda i, o: (0, 0, 0)),
            ],
            out_specs=pl.BlockSpec((per, width, columns), lambda i, o: (i, 0, 0)),
            scratch_shapes=[pltpu.VMEM((blocks, width, 2 * columns), jnp.bfloat16)],
        ),
        compiler_params=pltpu.CompilerParams(vmem_limit_bytes=24 * 2**20),
        cost_estimate=cost(tiles, 2),
        name="forward_product",
    )(offsets, tiles, far.reshape(blocks, width, columns))


def backward_product(tiles, offsets, near, exact):
    blocks, kept, width, _ = tiles.shape
    columns = near.shape[-1]
    per = ROWS_PER_STEP
    return pl.pallas_call(
        functools.partial(backward_kernel, exact),
        out_shape=(
            jax.ShapeDtypeStruct((blocks, width, columns), jnp.float32),
            jax.ShapeDtypeStruct((1, columns), jnp.float32),
        ),
        grid_spec=pltpu.PrefetchScalarGridSpec(
            num_scalar_prefetch=1,
            grid=(blocks // per,),
            in_specs=[
                pl.BlockSpec((per, kept, width, width), lambda i, o: (i, 0, 0, 0)),
                pl.BlockSpec((per, width, columns), lambda i, o: (i, 0, 0)),
            ],
            out_specs=(
                pl.BlockSpec((blocks, width, columns), lambda i, o: (0, 0, 0)),
                pl.BlockSpec((1, columns), lambda i, o: (0, 0)),
            ),
            scratch_shapes=[pltpu.VMEM((blocks, columns, width), jnp.float32)],
        ),
        compiler_params=pltpu.CompilerParams(vmem_limit_bytes=24 * 2**20),
        cost_estimate=cost(tiles, 2 if exact else 1),
        name="backward_product",
    )(offsets, tiles, near.reshape(blocks, width, columns))


def permute(value, place):
    rows, cols = lax.axis_size("row"), lax.axis_size("col")
    pairs = []
    for r in range(rows):
        for c in range(cols):
            to_row, to_col = place(r, c)
            pairs.append((r * cols + c, to_row % rows * cols + to_col % cols))
    return lax.ppermute(value, ("row", "col"), pairs)


def fetch_segment(value):
    half = lax.axis_size("col") // 2
    return permute(value, lambda r, c: (r - (c ^ half), c ^ half))


def return_segment(value):
    half = lax.axis_size("col") // 2
    return permute(value, lambda r, c: (r + c, c ^ half))


def sum_blocks(partial):
    count = lax.axis_size("col")
    rows, columns = partial.shape
    parts = partial.reshape(count, rows // count, columns)
    parts = lax.all_to_all(parts, "col", 0, 0)
    share = jnp.sum(parts.astype(jnp.float32), axis=0).astype(WIRE)
    copies = jnp.broadcast_to(share[None], parts.shape)
    return lax.all_to_all(copies, "col", 0, 0).reshape(rows, columns)


def row_values(*values):
    own = jnp.stack(values)
    copies = jnp.broadcast_to(own[None], (lax.axis_size("row"),) + own.shape)
    found = lax.all_to_all(copies, "row", 0, 0)
    return [found[:, k] for k in range(len(values))]


def pick(values, index):
    return lax.dynamic_index_in_dim(values, index, 0, keepdims=True)


def safe_ratio(top, bottom):
    return jnp.where(bottom > 0, top / jnp.where(bottom > 0, bottom, 1.0), 0.0)


def combine(products, residuals, weights, count):
    alpha = jnp.sum(products, axis=0) / count
    shift = safe_ratio(products, weights) - alpha
    mean_square = jnp.sum(residuals + shift * shift * weights, axis=0) / count
    return alpha, jnp.sqrt(mean_square + EPS)


def body(start_block, tiles, band_offsets):
    rows, cols = lax.axis_size("row"), lax.axis_size("col")
    row, col = lax.axis_index("row"), lax.axis_index("col")
    height, columns = start_block.shape
    count = height * rows
    tiles_dev = tiles[0, 0]
    offsets = band_offsets[0, 0]
    far_row = (row + col) % rows
    back_row = (row - (col ^ (cols // 2))) % rows

    def scale_of(squares):
        return lax.rsqrt(squares * (1.0 / height) + TINY)

    own_scale = scale_of(jnp.sum(start_block * start_block, axis=0))
    far = fetch_segment((start_block * (own_scale * SEGMENT_SCALE)).astype(WIRE))
    back, squares = backward_product(tiles_dev, offsets, start_block, True)
    back = return_segment(back.reshape(height, columns).astype(WIRE))
    (start_squares,) = row_values(squares[0])
    norm = jnp.sqrt(jnp.sum(start_squares, axis=0) / count + EPS)
    unit = (PRODUCT_SCALE / SEGMENT_SCALE) / (scale_of(start_squares) * norm)
    forward = forward_product(tiles_dev, offsets, far.astype(jnp.float32))
    back_unit = pick(unit, back_row)
    first = forward.reshape(height, columns) * pick(unit, far_row) + back.astype(jnp.float32) * back_unit
    first = first.astype(WIRE)
    product = sum_blocks(first)

    far = fetch_segment(product)
    near = product.astype(jnp.float32)
    back, squares = backward_product(tiles_dev, offsets, near, False)
    back = return_segment(back.reshape(height, columns).astype(WIRE))
    q_first = start_block / norm
    w_first = near * (1.0 / PRODUCT_SCALE)
    weights = start_squares / (norm * norm)
    own_weight = pick(weights, row)[0]
    inner = jnp.sum(q_first * w_first, axis=0)
    rest = w_first - safe_ratio(inner, own_weight) * q_first
    residual = jnp.sum(rest * rest, axis=0)
    squares, inner, residual = row_values(squares[0], inner, residual)
    alpha_one, beta_one = combine(inner, residual, weights, count)
    forward = forward_product(tiles_dev, offsets, far.astype(jnp.float32))
    back_unit = 1.0 / (SEGMENT_SCALE * pick(scale_of(squares), back_row))
    second = forward.reshape(height, columns) + back.astype(jnp.float32) * back_unit
    second = (second - alpha_one * first.astype(jnp.float32)) / beta_one
    product = sum_blocks(second.astype(WIRE))

    q_second = (w_first - alpha_one * q_first) / beta_one
    w_second = product.astype(jnp.float32) * (1.0 / PRODUCT_SCALE) - beta_one * q_first
    inner = jnp.sum(q_second * w_second, axis=0)
    weight = jnp.sum(q_second * q_second, axis=0)
    rest = w_second - safe_ratio(inner, weight) * q_second
    residual = jnp.sum(rest * rest, axis=0)
    inner, residual, weight = row_values(inner, residual, weight)
    alpha_two, beta_two = combine(inner, residual, weight, count)
    q_third = (w_second - alpha_two * q_second) / beta_two
    return (jnp.stack([alpha_one, alpha_two]), jnp.stack([beta_one, beta_two]), q_third)


def solution(mesh):
    placed = (P("row", None), P("row", "col", None, None, None, None), P("row", "col", None))
    return jax.shard_map(
        body, mesh=mesh, in_specs=placed, out_specs=(P(), P(), P("row", None)), check_vma=False
    )
```

```python
import functools

import jax
import jax.numpy as jnp
from jax import lax
from jax.experimental import pallas as pl
from jax.experimental.pallas import tpu as pltpu
from jax.sharding import PartitionSpec as P

EPS = 1e-06
TINY = 1e-30
WIRE = jnp.float16
PRODUCT_SCALE = 128.0
SEGMENT_SCALE = 1024.0
ROWS_PER_STEP = 2
VMEM_LIMIT = 56 * 2**20


def split_halves(value):
    high = value.astype(jnp.bfloat16)
    low = (value - high.astype(jnp.float32)).astype(jnp.bfloat16)
    return jnp.concatenate([high, low], axis=1)


def forward_kernel(places, tiles, near_half, far_half, out, halves):
    step = pl.program_id(0)
    blocks, width, columns = halves.shape[0], halves.shape[1], near_half.shape[2]
    each = blocks // 2
    kept = tiles.shape[1]
    start = places[kept] * each

    @pl.when(step == 0)
    def _():
        for block in range(each):
            halves[start + block] = split_halves(near_half[block])
            halves[each - start + block] = split_halves(far_half[block])

    for local in range(tiles.shape[0]):
        row = each - start + step * tiles.shape[0] + local
        total = jnp.zeros((width, 2 * columns), jnp.float32)
        for k in range(0, kept, 2):
            first = halves[lax.rem(row + places[k], blocks)]
            second = halves[lax.rem(row + places[k + 1], blocks)]
            left = jnp.concatenate([tiles[local, k], tiles[local, k + 1]], axis=1)
            right = jnp.concatenate([first, second], axis=0)
            total += jnp.dot(left, right, preferred_element_type=jnp.float32)
        out[local] = total[:, :columns] + total[:, columns:]


def backward_kernel(exact, places, tiles, near, out, squares, total):
    step = pl.program_id(0)
    blocks, columns, width = total.shape
    each = blocks // 2
    kept = tiles.shape[1]
    start = places[kept] * each

    @pl.when(step == 0)
    def _():
        total[...] = jnp.zeros_like(total)
        squares[...] = jnp.zeros_like(squares)

    for local in range(tiles.shape[0]):
        row = start + step * tiles.shape[0] + local
        value = near[local]
        squares[...] += jnp.sum(value * value, axis=0, keepdims=True)
        turned = value.T
        high = turned.astype(jnp.bfloat16)
        if exact:
            low = (turned - high.astype(jnp.float32)).astype(jnp.bfloat16)
            left = jnp.concatenate([high, low], axis=0)
        else:
            left = high
        for k in range(0, kept, 2):
            right = jnp.concatenate([tiles[local, k], tiles[local, k + 1]], axis=1)
            part = jnp.dot(left, right, preferred_element_type=jnp.float32)
            if exact:
                part = part[:columns] + part[columns:]
            total[lax.rem(row + places[k], blocks)] += part[:, :width]
            total[lax.rem(row + places[k + 1], blocks)] += part[:, width:]

    @pl.when(step == pl.num_programs(0) - 1)
    def _():
        rows = blocks * width
        scale = SEGMENT_SCALE * lax.rsqrt(squares[...] * (1.0 / rows) + TINY)
        for block in range(blocks):
            out[block] = total[lax.rem(start + block, blocks)].T * scale


def cost(tiles):
    return pl.CostEstimate(flops=0, bytes_accessed=tiles.size // 16, transcendentals=0)


def forward_product(tiles, places, own_half, other_half):
    blocks, kept, width, _ = tiles.shape
    columns = own_half.shape[-1]
    each = blocks // 2
    per = ROWS_PER_STEP
    steps = blocks // per
    whole = pl.BlockSpec((each, width, columns), lambda i, p: (0, 0, 0))
    out = pl.pallas_call(
        forward_kernel,
        out_shape=jax.ShapeDtypeStruct((blocks, width, columns), jnp.float32),
        grid_spec=pltpu.PrefetchScalarGridSpec(
            num_scalar_prefetch=1,
            grid=(steps,),
            in_specs=[
                pl.BlockSpec(
                    (per, kept, width, width),
                    lambda i, p: (lax.rem(i + (1 - p[kept]) * (steps // 2), steps), 0, 0, 0),
                ),
                whole,
                whole,
            ],
            out_specs=pl.BlockSpec((per, width, columns), lambda i, p: (i, 0, 0)),
            scratch_shapes=[pltpu.VMEM((blocks, width, 2 * columns), jnp.bfloat16)],
        ),
        compiler_params=pltpu.CompilerParams(vmem_limit_bytes=VMEM_LIMIT),
        cost_estimate=cost(tiles),
        name="forward_product",
    )(places, tiles, own_half.reshape(each, width, columns), other_half.reshape(each, width, columns))
    return out[:each].reshape(each * width, columns), out[each:].reshape(each * width, columns)


def backward_product(tiles, places, near, turn, exact):
    blocks, kept, width, _ = tiles.shape
    columns = near.shape[-1]
    each = blocks // 2
    per = ROWS_PER_STEP
    steps = blocks // per

    def block(i, p):
        return lax.rem(i + p[kept] * (steps // 2), steps)

    out = pl.pallas_call(
        functools.partial(backward_kernel, exact),
        out_shape=(
            jax.ShapeDtypeStruct((blocks, width, columns), jnp.float32),
            jax.ShapeDtypeStruct((1, columns), jnp.float32),
        ),
        grid_spec=pltpu.PrefetchScalarGridSpec(
            num_scalar_prefetch=1,
            grid=(steps,),
            in_specs=[
                pl.BlockSpec((per, kept, width, width), lambda i, p: (block(i, p), 0, 0, 0)),
                pl.BlockSpec(
                    (per, width, columns), lambda i, p: (i if turn else block(i, p), 0, 0)
                ),
            ],
            out_specs=(
                pl.BlockSpec((blocks, width, columns), lambda i, p: (0, 0, 0)),
                pl.BlockSpec((1, columns), lambda i, p: (0, 0)),
            ),
            scratch_shapes=[pltpu.VMEM((blocks, columns, width), jnp.float32)],
        ),
        compiler_params=pltpu.CompilerParams(vmem_limit_bytes=VMEM_LIMIT),
        cost_estimate=cost(tiles),
        name="backward_product",
    )(places, tiles, near.reshape(blocks, width, columns))[0]
    return out[:each].reshape(each * width, columns), out[each:].reshape(each * width, columns)


AXES = ("row", "half", "line")


def permute(value, place):
    rows = lax.axis_size("row")
    cols = lax.axis_size("half") * lax.axis_size("line")
    pairs = []
    for r in range(rows):
        for c in range(cols):
            to_row, to_col = place(r, c, c ^ (cols // 2))
            pairs.append((r * cols + c, to_row % rows * cols + to_col))
    return lax.ppermute(value, AXES, pairs)


def swap(value):
    return permute(value, lambda r, c, o: (r, o))


def fetch(value):
    own = permute(value, lambda r, c, o: (r - c, c))
    return own, permute(value, lambda r, c, o: (r - o, o))


def give_back(own, other):
    same = permute(own, lambda r, c, o: (r + c, c))
    return same, permute(other, lambda r, c, o: (r + c, o))


def sum_line(partial):
    count = lax.axis_size("line")
    rows, columns = partial.shape
    parts = partial.reshape(count, rows // count, columns)
    parts = lax.all_to_all(parts, "line", 0, 0)
    share = jnp.sum(parts.astype(jnp.float32), axis=0).astype(WIRE)
    copies = jnp.broadcast_to(share[None], parts.shape)
    return lax.all_to_all(copies, "line", 0, 0).reshape(rows, columns)


def segment_values(*values):
    own = jnp.stack(values)
    rows = lax.axis_size("row")
    copies = jnp.broadcast_to(own[None], (2 * rows,) + own.shape)
    found = lax.all_to_all(copies, ("row", "half"), 0, 0).reshape((rows, 2) + own.shape)
    return [found[:, :, k] for k in range(len(values))]


def pick(values, index):
    return lax.dynamic_index_in_dim(values, index, 0, keepdims=True)


def safe_ratio(top, bottom):
    return jnp.where(bottom > 0, top / jnp.where(bottom > 0, bottom, 1.0), 0.0)


def residual_of(vector, weight, product):
    inner = jnp.sum(vector * product, axis=0)
    rest = product - safe_ratio(inner, weight) * vector
    return inner, jnp.sum(rest * rest, axis=0)


def combine(inner, residual, weight, count):
    alpha = jnp.sum(inner, axis=(0, 1)) / count
    shift = safe_ratio(inner, weight) - alpha
    mean_square = jnp.sum(residual + shift * shift * weight, axis=(0, 1)) / count
    return alpha, jnp.sqrt(mean_square + EPS)


def wide(value):
    return value.astype(jnp.float32)


def body(start_block, tiles, band_offsets):
    rows, cols = lax.axis_size("row"), lax.axis_size("half") * lax.axis_size("line")
    row, half, line = lax.axis_index("row"), lax.axis_index("half"), lax.axis_index("line")
    col = half * (cols // 2) + line
    partner = (1 - half) * (cols // 2) + line
    height, columns = start_block.shape
    count = height * rows
    tiles_dev = tiles[0, 0]
    places = jnp.concatenate([band_offsets[0, 0], half[None].astype(jnp.int32)])
    far_row, partner_far_row = lax.rem(row + col, rows), lax.rem(row + partner, rows)
    back_row = lax.rem(row + cols - col, rows)
    partner_back_row = lax.rem(row + cols - partner, rows)
    start_half = lax.dynamic_slice_in_dim(start_block, half * (height // 2), height // 2, 0)

    def scale_of(squares):
        return lax.rsqrt(squares * (1.0 / height) + TINY)

    def ordered(own, other):
        first = jnp.where(half == 0, own, other)
        second = jnp.where(half == 0, other, own)
        return jnp.concatenate([first, second], axis=0)

    own_scale = scale_of(jnp.sum(start_block * start_block, axis=0))
    far = fetch((start_half * (own_scale * SEGMENT_SCALE)).astype(WIRE))
    start_weight = jnp.sum(start_half * start_half, axis=0)
    own, other = backward_product(tiles_dev, places, start_block, False, True)
    own, other, start_weight = lax.optimization_barrier(
        (own.astype(WIRE), other.astype(WIRE), start_weight)
    )
    back = give_back(own, other)
    (weights,) = segment_values(start_weight)
    norm = jnp.sqrt(jnp.sum(weights, axis=(0, 1)) / count + EPS)
    unit = (PRODUCT_SCALE / SEGMENT_SCALE) / (scale_of(jnp.sum(weights, axis=1)) * norm)
    weights = weights / (norm * norm)
    other, own = forward_product(tiles_dev, places, wide(far[0]), wide(far[1]))
    given = swap(other.astype(WIRE))
    first = own * pick(unit, far_row) + wide(given) * pick(unit, partner_far_row)
    first += wide(back[0]) * pick(unit, back_row) + wide(back[1]) * pick(unit, partner_back_row)
    first = first.astype(WIRE)
    product_half = sum_line(first)

    product_rest = swap(product_half)
    far = fetch(product_half)
    near = jnp.concatenate([wide(product_half), wide(product_rest)], axis=0)
    own, other = backward_product(tiles_dev, places, near, True, False)
    own, other, kept_half = lax.optimization_barrier((own.astype(WIRE), other.astype(WIRE), product_half))
    back = give_back(own, other)
    q_first = start_half / norm
    wide_half = wide(kept_half)
    w_first = wide_half * (1.0 / PRODUCT_SCALE)
    weight = start_weight / (norm * norm)
    inner, residual = residual_of(q_first, weight, w_first)
    squares = jnp.sum(wide_half * wide_half, axis=0)
    squares, inner, residual = segment_values(squares, inner, residual)
    alpha_one, beta_one = combine(inner, residual, weights, count)
    scale = SEGMENT_SCALE * scale_of(jnp.sum(squares, axis=1))
    unit = 1.0 / scale
    other, own = forward_product(tiles_dev, places, wide(far[0]), wide(far[1]))
    given = swap((other * pick(scale, far_row)).astype(WIRE))
    second = own + wide(given) * pick(unit, partner_far_row)
    second += wide(back[0]) * pick(unit, back_row) + wide(back[1]) * pick(unit, partner_back_row)
    second = (second - alpha_one * wide(first)) / beta_one
    last_half = sum_line(second.astype(WIRE))

    last_rest = swap(last_half)
    q_second = (w_first - alpha_one * q_first) / beta_one
    w_second = wide(last_half) * (1.0 / PRODUCT_SCALE) - beta_one * q_first
    weight = jnp.sum(q_second * q_second, axis=0)
    inner, residual = residual_of(q_second, weight, w_second)
    inner, residual, weight = segment_values(inner, residual, weight)
    alpha_two, beta_two = combine(inner, residual, weight, count)
    alpha_two, last_rest = lax.optimization_barrier((alpha_two, last_rest))
    q_first = start_block / norm
    q_second = ordered(wide(product_half), wide(product_rest)) * (1.0 / PRODUCT_SCALE)
    q_second = (q_second - alpha_one * q_first) / beta_one
    w_second = ordered(wide(last_half), wide(last_rest)) * (1.0 / PRODUCT_SCALE) - beta_one * q_first
    q_third = (w_second - alpha_two * q_second) / beta_two
    return (jnp.stack([alpha_one, alpha_two]), jnp.stack([beta_one, beta_two]), q_third)


def solution(mesh):
    rows, cols = mesh.devices.shape
    parted = jax.sharding.Mesh(mesh.devices.reshape(rows, 2, cols // 2), AXES)
    split = ("half", "line")
    placed = (P("row", None), P("row", split, None, None, None, None), P("row", split, None))
    return jax.shard_map(
        body, mesh=parted, in_specs=placed, out_specs=(P(), P(), P("row", None)), check_vma=False
    )
```

```python
import functools

import jax
import jax.numpy as jnp
from jax import lax
from jax.experimental import pallas as pl
from jax.experimental.pallas import tpu as pltpu
from jax.sharding import PartitionSpec as P

EPS = 1e-06
TINY = 1e-30
WIRE = jnp.float16
PRODUCT_SCALE = 128.0
SEGMENT_SCALE = 1024.0
ROWS_PER_STEP = 2
VMEM_LIMIT = 24 * 2**20
LOADING_VMEM_LIMIT = 53 * 2**20


def whole_vmem():
    return pl.BlockSpec(memory_space=pltpu.VMEM)


def whole_smem():
    return pl.BlockSpec(memory_space=pltpu.SMEM)


def low_part(value, high):
    return (value - high.astype(jnp.float32)).astype(jnp.bfloat16)


def forward_rows(begin, offsets, tiles, halves, out, factor):
    blocks, width, columns = halves.shape
    columns = columns // 2
    kept = tiles.shape[1]

    @pl.loop(0, out.shape[0] // ROWS_PER_STEP)
    def _(step):
        for local in range(ROWS_PER_STEP):
            at = step * ROWS_PER_STEP + local
            row = begin + at
            total = jnp.zeros((width, 2 * columns), jnp.float32)
            for k in range(0, kept, 2):
                first = halves[lax.rem(row + offsets[k], blocks)]
                second = halves[lax.rem(row + offsets[k + 1], blocks)]
                left = jnp.concatenate([tiles[row, k], tiles[row, k + 1]], axis=1)
                right = jnp.concatenate([first, second], axis=0)
                total += jnp.dot(left, right, preferred_element_type=jnp.float32)
            result = total[:, :columns] + total[:, columns:]
            out[at] = result if factor is None else result * factor


def forward_first_kernel(offsets, half, tiles, own_half, other_half, out, halves):
    each, width, columns = own_half.shape
    start = half[0] * each
    squares = jnp.zeros((1, columns), jnp.float32)
    for block in range(each):
        for source, base in ((own_half, start), (other_half, each - start)):
            value = source[block]
            squares += jnp.sum(value * value, axis=0, keepdims=True)
            high = value.astype(jnp.bfloat16)
            halves[base + block] = jnp.concatenate([high, low_part(value, high)], axis=1)
    factor = SEGMENT_SCALE * lax.rsqrt(squares * (0.5 / (each * width)) + TINY)
    forward_rows(each - start, offsets, tiles, halves, out, factor)


def forward_second_kernel(offsets, half, tiles, halves, out):
    forward_rows(half[0] * out.shape[0], offsets, tiles, halves, out, None)


def backward_rows(row, exact, offsets, tiles, value, squares, total):
    blocks, columns, width = total.shape
    squares[...] += jnp.sum(value * value, axis=0, keepdims=True)
    turned = value.T
    left = turned.astype(jnp.bfloat16)
    if exact:
        left = jnp.concatenate([left, low_part(turned, left)], axis=0)
    for k in range(0, tiles.shape[1], 2):
        right = jnp.concatenate([tiles[row, k], tiles[row, k + 1]], axis=1)
        part = jnp.dot(left, right, preferred_element_type=jnp.float32)
        if exact:
            part = part[:columns] + part[columns:]
        total[lax.rem(row + offsets[k], blocks)] += part[:, :width]
        total[lax.rem(row + offsets[k + 1], blocks)] += part[:, width:]


def backward_result(start, squares, total, given, out):
    blocks, _, width = total.shape
    scale = SEGMENT_SCALE * lax.rsqrt(squares * (1.0 / (blocks * width)) + TINY)
    for block in range(blocks):
        place = lax.rem(start + block, blocks)
        value = total[place] if given is None else total[place] + given[place]
        out[block] = value.T * scale


def backward_loading_kernel(offsets, half, source, near, out, tiles, squares, total, arrived):
    blocks = total.shape[0]
    start = half[0] * (blocks // 2)
    steps = blocks // ROWS_PER_STEP

    def load(step):
        part = pl.ds(step * ROWS_PER_STEP, ROWS_PER_STEP)
        return pltpu.make_async_copy(source.at[part], tiles.at[part], arrived.at[step])

    for step in range(steps):
        load(step).start()
    total[...] = jnp.zeros_like(total)
    squares[...] = jnp.zeros_like(squares)

    @pl.loop(0, steps)
    def _(step):
        load(step).wait()
        for local in range(ROWS_PER_STEP):
            row = step * ROWS_PER_STEP + local
            backward_rows(row, True, offsets, tiles, near[row], squares, total)

    backward_result(start, squares[...], total, None, out)


def backward_first_kernel(offsets, half, tiles, near, total, squares):
    each = near.shape[0]
    total[...] = jnp.zeros_like(total)
    squares[...] = jnp.zeros_like(squares)

    @pl.loop(0, each // ROWS_PER_STEP)
    def _(step):
        for local in range(ROWS_PER_STEP):
            at = step * ROWS_PER_STEP + local
            row = half[0] * each + at
            backward_rows(row, False, offsets, tiles, near[at], squares, total)


def backward_second_kernel(offsets, half, tiles, near, given, given_squares, out, squares, total):
    each = near.shape[0]
    total[...] = jnp.zeros_like(total)
    squares[...] = given_squares[...]

    @pl.loop(0, each // ROWS_PER_STEP)
    def _(step):
        for local in range(ROWS_PER_STEP):
            at = step * ROWS_PER_STEP + local
            row = (1 - half[0]) * each + at
            backward_rows(row, False, offsets, tiles, near[at], squares, total)

    backward_result(half[0] * each, squares[...], total, given, out)


def call(kernel, name, out_shape, scratch, offsets, half, tiles, *values):
    loading = kernel is backward_loading_kernel
    tiles_spec = pl.BlockSpec(memory_space=pl.ANY) if loading else whole_vmem()
    return pl.pallas_call(
        kernel,
        out_shape=out_shape,
        in_specs=[whole_smem(), whole_smem(), tiles_spec] + [whole_vmem()] * len(values),
        out_specs=tuple(whole_vmem() for _ in out_shape),
        scratch_shapes=scratch or [],
        compiler_params=pltpu.CompilerParams(vmem_limit_bytes=LOADING_VMEM_LIMIT if loading else VMEM_LIMIT),
        cost_estimate=pl.CostEstimate(flops=0, bytes_accessed=2**16, transcendentals=0),
        name=name,
    )(offsets, half, tiles, *values)


def forward_product(tiles, offsets, half, own_half, other_half):
    blocks, _, width, _ = tiles.shape
    columns = own_half.shape[-1]
    each = blocks // 2
    shape = (each, width, columns)
    part = jax.ShapeDtypeStruct(shape, jnp.float32)
    other, halves = call(
        forward_first_kernel,
        "forward_first",
        (part, pltpu.VMEM((blocks, width, 2 * columns), jnp.bfloat16)),
        None,
        offsets, half, tiles, own_half.reshape(shape), other_half.reshape(shape),
    )
    (own,) = call(forward_second_kernel, "forward_second", (part,), None, offsets, half, tiles, halves)
    return other.reshape(each * width, columns), own.reshape(each * width, columns)


def in_halves(value):
    each = value.shape[0] // 2
    value = value.reshape(2, each * value.shape[1], value.shape[2])
    return value[0].astype(WIRE), value[1].astype(WIRE)


def backward_loading(tiles, offsets, half, near):
    blocks, _, width, _ = tiles.shape
    columns = near.shape[-1]
    shape = (blocks, width, columns)
    out, kept = call(
        backward_loading_kernel,
        "backward_loading",
        (pltpu.VMEM(shape, jnp.float32), pltpu.VMEM(tiles.shape, tiles.dtype)),
        [
            pltpu.VMEM((1, columns), jnp.float32),
            pltpu.VMEM((blocks, columns, width), jnp.float32),
            pltpu.SemaphoreType.DMA((blocks // ROWS_PER_STEP,)),
        ],
        offsets, half, tiles, near.reshape(shape),
    )
    return in_halves(out), kept


def backward_product(tiles, offsets, half, own_half, other_half):
    blocks, _, width, _ = tiles.shape
    columns = own_half.shape[-1]
    shape = (blocks // 2, width, columns)
    total = (blocks, columns, width)
    given, squares = call(
        backward_first_kernel,
        "backward_first",
        (jax.ShapeDtypeStruct(total, jnp.float32), jax.ShapeDtypeStruct((1, columns), jnp.float32)),
        None,
        offsets, half, tiles, own_half.reshape(shape),
    )
    (out,) = call(
        backward_second_kernel,
        "backward_second",
        (jax.ShapeDtypeStruct((blocks, width, columns), jnp.float32),),
        [pltpu.VMEM((1, columns), jnp.float32), pltpu.VMEM(total, jnp.float32)],
        offsets, half, tiles, other_half.reshape(shape), given, squares,
    )
    return in_halves(out)


AXES = ("row", "half", "line")


def permute(value, place):
    rows = lax.axis_size("row")
    cols = lax.axis_size("half") * lax.axis_size("line")
    pairs = []
    for r in range(rows):
        for c in range(cols):
            to_row, to_col = place(r, c, c ^ (cols // 2))
            pairs.append((r * cols + c, to_row % rows * cols + to_col))
    return lax.ppermute(value, AXES, pairs)


def swap(value):
    return permute(value, lambda r, c, o: (r, o))


def fetch(value):
    own = permute(value, lambda r, c, o: (r - c, c))
    return own, permute(value, lambda r, c, o: (r - o, o))


def give_back(own, other):
    same = permute(own, lambda r, c, o: (r + c, c))
    return same, permute(other, lambda r, c, o: (r + c, o))


def sum_line(partial):
    count = lax.axis_size("line")
    rows, columns = partial.shape
    parts = partial.reshape(count, rows // count, columns)
    parts = lax.all_to_all(parts, "line", 0, 0)
    share = jnp.sum(parts.astype(jnp.float32), axis=0).astype(WIRE)
    copies = jnp.broadcast_to(share[None], parts.shape)
    return lax.all_to_all(copies, "line", 0, 0).reshape(rows, columns)


def segment_values(*values):
    own = jnp.stack(values)
    rows = lax.axis_size("row")
    copies = jnp.broadcast_to(own[None], (2 * rows,) + own.shape)
    found = lax.all_to_all(copies, ("row", "half"), 0, 0).reshape((rows, 2) + own.shape)
    return [found[:, :, k] for k in range(len(values))]


def pick(values, index):
    return lax.dynamic_index_in_dim(values, index, 0, keepdims=True)


def safe_ratio(top, bottom):
    return jnp.where(bottom > 0, top / jnp.where(bottom > 0, bottom, 1.0), 0.0)


def residual_of(vector, weight, product):
    inner = jnp.sum(vector * product, axis=0)
    rest = product - safe_ratio(inner, weight) * vector
    return inner, jnp.sum(rest * rest, axis=0)


def combine(inner, residual, weight, count):
    alpha = jnp.sum(inner, axis=(0, 1)) / count
    shift = safe_ratio(inner, weight) - alpha
    mean_square = jnp.sum(residual + shift * shift * weight, axis=(0, 1)) / count
    return alpha, jnp.sqrt(mean_square + EPS)


def wide(value):
    return value.astype(jnp.float32)


def body(start_block, tiles, band_offsets):
    rows, cols = lax.axis_size("row"), lax.axis_size("half") * lax.axis_size("line")
    row, half, line = lax.axis_index("row"), lax.axis_index("half"), lax.axis_index("line")
    col = half * (cols // 2) + line
    partner = (1 - half) * (cols // 2) + line
    height, columns = start_block.shape
    count = height * rows
    offsets = band_offsets[0, 0]
    place = half[None].astype(jnp.int32)
    far_row, partner_far_row = lax.rem(row + col, rows), lax.rem(row + partner, rows)
    back_row = lax.rem(row + cols - col, rows)
    partner_back_row = lax.rem(row + cols - partner, rows)
    start_half = lax.dynamic_slice_in_dim(start_block, half * (height // 2), height // 2, 0)

    def scale_of(squares):
        return lax.rsqrt(squares * (1.0 / height) + TINY)

    def ordered(own, other):
        first = jnp.where(half == 0, own, other)
        second = jnp.where(half == 0, other, own)
        return jnp.concatenate([first, second], axis=0)

    own_scale = scale_of(jnp.sum(start_block * start_block, axis=0))
    far_own, far_other = fetch((start_half * (own_scale * SEGMENT_SCALE)).astype(WIRE))
    back, kept = backward_loading(tiles[0, 0], offsets, place, start_block)
    back = give_back(*back)
    start_weight = jnp.sum(start_half * start_half, axis=0)
    far_own, start_weight = lax.optimization_barrier((far_own, start_weight))
    (weights,) = segment_values(start_weight)
    norm = jnp.sqrt(jnp.sum(weights, axis=(0, 1)) / count + EPS)
    unit = (PRODUCT_SCALE / SEGMENT_SCALE) / (scale_of(jnp.sum(weights, axis=1)) * norm)
    weights = weights / (norm * norm)
    other, own = forward_product(kept, offsets, place, wide(far_own), wide(far_other))
    given = swap(other.astype(WIRE))
    first = own * pick(unit, far_row) + wide(given) * pick(unit, partner_far_row)
    first += wide(back[0]) * pick(unit, back_row) + wide(back[1]) * pick(unit, partner_back_row)
    first = first.astype(WIRE)
    product_half = sum_line(first)

    product_rest = swap(product_half)
    far_own, far_other = fetch(product_half)
    back = give_back(
        *backward_product(kept, offsets, place, wide(product_half), wide(product_rest))
    )
    far_own, kept_half = lax.optimization_barrier((far_own, product_half))
    q_first = start_half / norm
    wide_half = wide(kept_half)
    w_first = wide_half * (1.0 / PRODUCT_SCALE)
    weight = start_weight / (norm * norm)
    inner, residual = residual_of(q_first, weight, w_first)
    squares = jnp.sum(wide_half * wide_half, axis=0)
    squares, inner, residual = segment_values(squares, inner, residual)
    alpha_one, beta_one = combine(inner, residual, weights, count)
    unit = 1.0 / (SEGMENT_SCALE * scale_of(jnp.sum(squares, axis=1)))
    other, own = forward_product(kept, offsets, place, wide(far_own), wide(far_other))
    given = swap(other.astype(WIRE))
    second = own + wide(given) * pick(unit, partner_far_row)
    second += wide(back[0]) * pick(unit, back_row) + wide(back[1]) * pick(unit, partner_back_row)
    second = (second - alpha_one * wide(first)) / beta_one
    last_half = sum_line(second.astype(WIRE))

    last_rest = swap(last_half)
    q_second = (w_first - alpha_one * q_first) / beta_one
    w_second = wide(last_half) * (1.0 / PRODUCT_SCALE) - beta_one * q_first
    weight = jnp.sum(q_second * q_second, axis=0)
    inner, residual = residual_of(q_second, weight, w_second)
    inner, residual, weight = segment_values(inner, residual, weight)
    alpha_two, beta_two = combine(inner, residual, weight, count)
    q_first = start_block / norm
    q_second = ordered(wide(product_half), wide(product_rest)) * (1.0 / PRODUCT_SCALE)
    q_second = (q_second - alpha_one * q_first) / beta_one
    w_second = ordered(wide(last_half), wide(last_rest)) * (1.0 / PRODUCT_SCALE) - beta_one * q_first
    q_third = (w_second - alpha_two * q_second) / beta_two
    return (jnp.stack([alpha_one, alpha_two]), jnp.stack([beta_one, beta_two]), q_third)


def solution(mesh):
    rows, cols = mesh.devices.shape
    parted = jax.sharding.Mesh(mesh.devices.reshape(rows, 2, cols // 2), AXES)
    split = ("half", "line")
    placed = (P("row", None), P("row", split, None, None, None, None), P("row", split, None))
    return jax.shard_map(
        body, mesh=parted, in_specs=placed, out_specs=(P(), P(), P("row", None)), check_vma=False
    )
```

```python
import functools

import jax
import jax.numpy as jnp
from jax import lax
from jax.experimental import pallas as pl
from jax.experimental.pallas import tpu as pltpu
from jax.sharding import PartitionSpec as P

EPS = 1e-06
TINY = 1e-30
WIRE = jnp.float16
SEGMENT_SCALE = 1024.0
PEAK_EXPONENT = 14.0
CODE_ROWS = 16
ROWS_PER_STEP = 2
VMEM_LIMIT = 24 * 2**20
LOADING_VMEM_LIMIT = 53 * 2**20


def whole_vmem():
    return pl.BlockSpec(memory_space=pltpu.VMEM)


def whole_smem():
    return pl.BlockSpec(memory_space=pltpu.SMEM)


def low_part(value, high):
    return (value - high.astype(jnp.float32)).astype(jnp.bfloat16)


def code_of(squares, rows):
    return jnp.floor(jnp.log2(SEGMENT_SCALE * lax.rsqrt(squares * (1.0 / rows) + TINY)))


def forward_rows(begin, offsets, tiles, halves, out, factor):
    blocks, width, columns = halves.shape
    columns = columns // 2
    kept = tiles.shape[1]

    @pl.loop(0, blocks // 2 // ROWS_PER_STEP)
    def _(step):
        for local in range(ROWS_PER_STEP):
            at = step * ROWS_PER_STEP + local
            row = begin + at
            total = jnp.zeros((width, 2 * columns), jnp.float32)
            for k in range(0, kept, 2):
                first = halves[lax.rem(row + offsets[k], blocks)]
                second = halves[lax.rem(row + offsets[k + 1], blocks)]
                left = jnp.concatenate([tiles[row, k], tiles[row, k + 1]], axis=1)
                right = jnp.concatenate([first, second], axis=0)
                total += jnp.dot(left, right, preferred_element_type=jnp.float32)
            result = total[:, :columns] + total[:, columns:]
            out[pl.ds(pl.multiple_of(at * width, width), width)] = (
                result if factor is None else result * factor
            )


def forward_first_kernel(offsets, half, tiles, own_half, other_half, out, halves):
    each, width, columns = own_half.shape
    start = half[0] * each
    squares = jnp.zeros((1, columns), jnp.float32)
    for block in range(each):
        for source, base in ((own_half, start), (other_half, each - start)):
            value = source[block]
            squares += jnp.sum(value * value, axis=0, keepdims=True)
            high = value.astype(jnp.bfloat16)
            halves[base + block] = jnp.concatenate([high, low_part(value, high)], axis=1)
    code = code_of(squares, 2 * each * width)
    out[each * width :] = jnp.broadcast_to(code, (CODE_ROWS, columns))
    forward_rows(each - start, offsets, tiles, halves, out, jnp.exp2(code))


def forward_second_kernel(offsets, half, tiles, halves, out):
    forward_rows(half[0] * (halves.shape[0] // 2), offsets, tiles, halves, out, None)


def backward_rows(row, offsets, tiles, value, squares, total):
    blocks, columns, width = total.shape
    squares[...] += jnp.sum(value * value, axis=0, keepdims=True)
    turned = value.T
    high = turned.astype(jnp.bfloat16)
    left = jnp.concatenate([high, low_part(turned, high)], axis=0)
    for k in range(0, tiles.shape[1], 2):
        right = jnp.concatenate([tiles[row, k], tiles[row, k + 1]], axis=1)
        part = jnp.dot(left, right, preferred_element_type=jnp.float32)
        part = part[:columns] + part[columns:]
        total[lax.rem(row + offsets[k], blocks)] += part[:, :width]
        total[lax.rem(row + offsets[k + 1], blocks)] += part[:, width:]


def backward_result(start, squares, total, given, out):
    blocks, columns, width = total.shape
    each = blocks // 2
    code = code_of(squares, blocks * width)
    scale = jnp.exp2(code)
    for block in range(blocks):
        place = lax.rem(start + block, blocks)
        value = total[place] if given is None else total[place] + given[place]
        at = block % each * width
        out[block // each, at : at + width] = value.T * scale
    for part in range(2):
        out[part, each * width :] = jnp.broadcast_to(code, (CODE_ROWS, columns))


def backward_loading_kernel(offsets, half, source, near, out, tiles, squares, total, arrived):
    blocks = total.shape[0]
    start = half[0] * (blocks // 2)
    steps = blocks // ROWS_PER_STEP

    def load(step):
        part = pl.ds(step * ROWS_PER_STEP, ROWS_PER_STEP)
        return pltpu.make_async_copy(source.at[part], tiles.at[part], arrived.at[step])

    for step in range(steps):
        load(step).start()
    total[...] = jnp.zeros_like(total)
    squares[...] = jnp.zeros_like(squares)

    @pl.loop(0, steps)
    def _(step):
        load(step).wait()
        for local in range(ROWS_PER_STEP):
            row = step * ROWS_PER_STEP + local
            backward_rows(row, offsets, tiles, near[row], squares, total)

    backward_result(start, squares[...], total, None, out)


def backward_first_kernel(offsets, half, tiles, near, total, squares):
    each = near.shape[0]
    total[...] = jnp.zeros_like(total)
    squares[...] = jnp.zeros_like(squares)

    @pl.loop(0, each // ROWS_PER_STEP)
    def _(step):
        for local in range(ROWS_PER_STEP):
            at = step * ROWS_PER_STEP + local
            row = half[0] * each + at
            backward_rows(row, offsets, tiles, near[at], squares, total)


def backward_second_kernel(offsets, half, tiles, near, given, given_squares, out, squares, total):
    each = near.shape[0]
    total[...] = jnp.zeros_like(total)
    squares[...] = given_squares[...]

    @pl.loop(0, each // ROWS_PER_STEP)
    def _(step):
        for local in range(ROWS_PER_STEP):
            at = step * ROWS_PER_STEP + local
            row = (1 - half[0]) * each + at
            backward_rows(row, offsets, tiles, near[at], squares, total)

    backward_result(half[0] * each, squares[...], total, given, out)


def gram_kernel(start, first, second, out):
    count, width, columns = start.shape

    def total(function):
        sums = jnp.zeros((width, columns), jnp.float32)
        for block in range(count):
            sums += function(start[block], first[block], second[block])
        return jnp.sum(sums, axis=0, keepdims=True)

    weight = total(lambda s, u, v: s * s)
    usable = weight > 0
    safe = jnp.where(usable, weight, 1.0)
    a = jnp.where(usable, total(lambda s, u, v: s * u) / safe, 0.0)
    b = jnp.where(usable, total(lambda s, u, v: s * (v - a * u)) / safe, 0.0)
    out[...] = jnp.zeros_like(out)
    out[0:1] = a
    out[1:2] = b
    out[2:3] = weight
    out[3:4] = total(lambda s, u, v: (u - a * s) * (u - a * s))
    out[4:5] = total(lambda s, u, v: (u - a * s) * (v - a * u - b * s))
    out[5:6] = total(lambda s, u, v: (v - a * u - b * s) * (v - a * u - b * s))


def scalar_kernel(count, found, out):
    a, b, weight, uu, uv, vv = (found[:, k, :] for k in range(6))

    def mean(value):
        return jnp.sum(value, axis=0, keepdims=True) * (1.0 / count)

    norm = jnp.sqrt(mean(weight) + EPS)
    inverse = 1.0 / norm
    alpha_one = mean(a * weight) * inverse * inverse
    delta = a - alpha_one
    beta_one = jnp.sqrt(mean(uu + delta * delta * weight) * inverse * inverse + EPS)
    k = inverse / beta_one
    shift = b + delta * a - beta_one * beta_one
    alpha_two = k * k * mean(uv + delta * uu + delta * shift * weight)
    along = delta - alpha_two
    rest = shift - alpha_two * delta
    square = mean(vv + 2.0 * along * uv + along * along * uu + rest * rest * weight)
    beta_two = jnp.sqrt(k * k * square + EPS)
    out[...] = jnp.zeros_like(out)
    out[0:1] = alpha_one
    out[1:2] = alpha_two
    out[2:3] = beta_one
    out[3:4] = beta_two
    out[4:5] = (k * alpha_one * alpha_two - beta_one * inverse) / beta_two
    out[5:6] = -k * (alpha_one + alpha_two) / beta_two
    out[6:7] = k / beta_two


def small_call(kernel, name, *values):
    columns = values[0].shape[-1]
    return pl.pallas_call(
        kernel,
        out_shape=jax.ShapeDtypeStruct((8, columns), jnp.float32),
        in_specs=[whole_vmem()] * len(values),
        out_specs=whole_vmem(),
        compiler_params=pltpu.CompilerParams(vmem_limit_bytes=VMEM_LIMIT),
        cost_estimate=pl.CostEstimate(flops=0, bytes_accessed=2**16, transcendentals=0),
        name=name,
    )(*values)


def call(kernel, name, out_shape, scratch, offsets, half, tiles, *values):
    loading = kernel is backward_loading_kernel
    tiles_spec = pl.BlockSpec(memory_space=pl.ANY) if loading else whole_vmem()
    return pl.pallas_call(
        kernel,
        out_shape=out_shape,
        in_specs=[whole_smem(), whole_smem(), tiles_spec] + [whole_vmem()] * len(values),
        out_specs=tuple(whole_vmem() for _ in out_shape),
        scratch_shapes=scratch or [],
        compiler_params=pltpu.CompilerParams(vmem_limit_bytes=LOADING_VMEM_LIMIT if loading else VMEM_LIMIT),
        cost_estimate=pl.CostEstimate(flops=0, bytes_accessed=2**16, transcendentals=0),
        name=name,
    )(offsets, half, tiles, *values)


def forward_product(tiles, offsets, half, own_half, other_half):
    blocks, _, width, _ = tiles.shape
    columns = own_half.shape[-1]
    each = blocks // 2
    shape = (each, width, columns)
    message = jax.ShapeDtypeStruct((each * width + CODE_ROWS, columns), jnp.float32)
    part = jax.ShapeDtypeStruct((each * width, columns), jnp.float32)
    other, halves = call(
        forward_first_kernel,
        "forward_first",
        (message, pltpu.VMEM((blocks, width, 2 * columns), jnp.bfloat16)),
        None,
        offsets, half, tiles, own_half.reshape(shape), other_half.reshape(shape),
    )
    (own,) = call(forward_second_kernel, "forward_second", (part,), None, offsets, half, tiles, halves)
    return other.astype(WIRE), own


def messages_shape(blocks, width, columns):
    return (2, blocks // 2 * width + CODE_ROWS, columns)


def two_messages(value):
    return value[0].astype(WIRE), value[1].astype(WIRE)


def backward_loading(tiles, offsets, half, near):
    blocks, _, width, _ = tiles.shape
    columns = near.shape[-1]
    shape = (blocks, width, columns)
    out, kept = call(
        backward_loading_kernel,
        "backward_loading",
        (
            pltpu.VMEM(messages_shape(blocks, width, columns), jnp.float32),
            pltpu.VMEM(tiles.shape, tiles.dtype),
        ),
        [
            pltpu.VMEM((1, columns), jnp.float32),
            pltpu.VMEM((blocks, columns, width), jnp.float32),
            pltpu.SemaphoreType.DMA((blocks // ROWS_PER_STEP,)),
        ],
        offsets, half, tiles, near.reshape(shape),
    )
    return two_messages(out), kept


def backward_product(tiles, offsets, half, own_half, other_half):
    blocks, _, width, _ = tiles.shape
    columns = own_half.shape[-1]
    shape = (blocks // 2, width, columns)
    total = (blocks, columns, width)
    given, squares = call(
        backward_first_kernel,
        "backward_first",
        (jax.ShapeDtypeStruct(total, jnp.float32), jax.ShapeDtypeStruct((1, columns), jnp.float32)),
        None,
        offsets, half, tiles, own_half.reshape(shape),
    )
    (out,) = call(
        backward_second_kernel,
        "backward_second",
        (jax.ShapeDtypeStruct(messages_shape(blocks, width, columns), jnp.float32),),
        [pltpu.VMEM((1, columns), jnp.float32), pltpu.VMEM(total, jnp.float32)],
        offsets, half, tiles, other_half.reshape(shape), given, squares,
    )
    return two_messages(out)


AXES = ("row", "half", "line")


def permute(value, place):
    rows = lax.axis_size("row")
    cols = lax.axis_size("half") * lax.axis_size("line")
    pairs = []
    for r in range(rows):
        for c in range(cols):
            to_row, to_col = place(r, c, c ^ (cols // 2))
            pairs.append((r * cols + c, to_row % rows * cols + to_col))
    return lax.ppermute(value, AXES, pairs)


def swap(value):
    return permute(value, lambda r, c, o: (r, o))


def fetch(value):
    own = permute(value, lambda r, c, o: (r - c, c))
    return own, permute(value, lambda r, c, o: (r - o, o))


def give_back(own, other):
    same = permute(own, lambda r, c, o: (r + c, c))
    return same, permute(other, lambda r, c, o: (r + c, o))


def encode(value):
    peak = jnp.max(jnp.abs(value), axis=-2, keepdims=True)
    code = PEAK_EXPONENT - jnp.floor(jnp.log2(jnp.maximum(peak, TINY)))
    codes = jnp.broadcast_to(code, value.shape[:-2] + (CODE_ROWS, value.shape[-1]))
    return jnp.concatenate([(value * jnp.exp2(code)).astype(WIRE), codes.astype(WIRE)], axis=-2)


def decode(message):
    rows = message.shape[-2] - CODE_ROWS
    value = message[..., :rows, :].astype(jnp.float32)
    return value * jnp.exp2(-message[..., rows : rows + 1, :].astype(jnp.float32))


def sum_line(partial):
    count = lax.axis_size("line")
    rows, columns = partial.shape
    parts = encode(partial.reshape(count, rows // count, columns))
    parts = lax.all_to_all(parts, "line", 0, 0)
    share = encode(jnp.sum(decode(parts), axis=0))
    return lax.all_to_all(jnp.broadcast_to(share[None], parts.shape), "line", 0, 0)


def segment_values(own):
    rows = lax.axis_size("row")
    copies = jnp.broadcast_to(own[None], (2 * rows,) + own.shape)
    return lax.all_to_all(copies, ("row", "half"), 0, 0)


def body(start_block, tiles, band_offsets):
    half = lax.axis_index("half")
    rows, height, columns = lax.axis_size("row"), *start_block.shape
    parts = lax.axis_size("line")
    offsets = band_offsets[0, 0]
    place = half[None].astype(jnp.int32)
    start_half = lax.dynamic_slice_in_dim(start_block, half * (height // 2), height // 2, 0)
    start_half = start_half.reshape(parts, height // 2 // parts, columns)

    def partial_sum(kept, far, back):
        other, own = forward_product(kept, offsets, place, decode(far[0]), decode(far[1]))
        given = swap(other)
        return own + decode(given) + decode(back[0]) + decode(back[1])

    def ordered(own, other):
        first = jnp.where(half == 0, own, other)
        second = jnp.where(half == 0, other, own)
        return jnp.concatenate([first, second], axis=0).reshape(height, columns)

    far = fetch(encode(start_half))
    back, kept = backward_loading(tiles[0, 0], offsets, place, start_block)
    first = sum_line(partial_sum(kept, far, give_back(*back)))

    first_rest = swap(first)
    far = fetch(first)
    first_half, first_rest = decode(first), decode(first_rest)
    back = backward_product(kept, offsets, place, first_half, first_rest)
    second = sum_line(partial_sum(kept, far, give_back(*back)))

    second_rest = swap(second)
    second_half = decode(second)
    found = segment_values(small_call(gram_kernel, "gram", start_half, first_half, second_half))
    scalars = small_call(functools.partial(scalar_kernel, height * rows), "scalars", found)
    scalars, second_rest = lax.optimization_barrier((scalars, second_rest))
    q_third = (
        scalars[4] * start_block
        + scalars[5] * ordered(first_half, first_rest)
        + scalars[6] * ordered(second_half, decode(second_rest))
    )
    return (scalars[0:2], scalars[2:4], q_third)


def solution(mesh):
    rows, cols = mesh.devices.shape
    parted = jax.sharding.Mesh(mesh.devices.reshape(rows, 2, cols // 2), AXES)
    split = ("half", "line")
    placed = (P("row", None), P("row", split, None, None, None, None), P("row", split, None))
    return jax.shard_map(
        body, mesh=parted, in_specs=placed, out_specs=(P(), P(), P("row", None)), check_vma=False
    )
```

```python
import functools

import jax
import jax.numpy as jnp
from jax import lax
from jax.experimental import pallas as pl
from jax.experimental.pallas import tpu as pltpu
from jax.sharding import PartitionSpec as P

EPS = 1e-06
TINY = 1e-30
WIRE = jnp.float16
SEGMENT_SCALE = 1024.0
PEAK_EXPONENT = 14.0
CODE_ROWS = 16
ROWS_PER_STEP = 8
VMEM_LIMIT = 24 * 2**20
LOADING_VMEM_LIMIT = 53 * 2**20


def whole_vmem():
    return pl.BlockSpec(memory_space=pltpu.VMEM)


def whole_smem():
    return pl.BlockSpec(memory_space=pltpu.SMEM)


def low_part(value, high):
    return (value - high.astype(jnp.float32)).astype(jnp.bfloat16)


def code_of(squares, rows):
    return jnp.floor(jnp.log2(SEGMENT_SCALE * lax.rsqrt(squares * (1.0 / rows) + TINY)))


def forward_rows(begin, offsets, tiles, halves, out, factor):
    blocks, width, columns = halves.shape
    columns = columns // 2
    kept = tiles.shape[1]

    @pl.loop(0, blocks // 2 // ROWS_PER_STEP)
    def _(step):
        for local in range(ROWS_PER_STEP):
            at = step * ROWS_PER_STEP + local
            row = begin + at
            total = jnp.zeros((width, 2 * columns), jnp.float32)
            for k in range(0, kept, 2):
                first = halves[(row + offsets[k]) & (blocks - 1)]
                second = halves[(row + offsets[k + 1]) & (blocks - 1)]
                left = jnp.concatenate([tiles[row, k], tiles[row, k + 1]], axis=1)
                right = jnp.concatenate([first, second], axis=0)
                total += jnp.dot(left, right, preferred_element_type=jnp.float32)
            result = total[:, :columns] + total[:, columns:]
            out[pl.ds(pl.multiple_of(at * width, width), width)] = (
                result if factor is None else result * factor
            )


def forward_first_kernel(offsets, half, tiles, own_half, other_half, out, halves):
    each, width, columns = own_half.shape
    start = half[0] * each
    squares = jnp.zeros((1, columns), jnp.float32)
    for block in range(each):
        for source, base in ((own_half, start), (other_half, each - start)):
            value = source[block]
            squares += jnp.sum(value * value, axis=0, keepdims=True)
            high = value.astype(jnp.bfloat16)
            halves[base + block] = jnp.concatenate([high, low_part(value, high)], axis=1)
    code = code_of(squares, 2 * each * width)
    out[each * width :] = jnp.broadcast_to(code, (CODE_ROWS, columns))
    forward_rows(each - start, offsets, tiles, halves, out, jnp.exp2(code))


def forward_second_kernel(offsets, half, tiles, halves, out):
    forward_rows(half[0] * (halves.shape[0] // 2), offsets, tiles, halves, out, None)


def turn_rows(block, value, squares, turned):
    squares[...] += jnp.sum(value * value, axis=0, keepdims=True)
    value = value.T
    high = value.astype(jnp.bfloat16)
    turned[block] = jnp.concatenate([high, low_part(value, high)], axis=0)


def backward_block(block, kinds, offsets, tiles, turned):
    blocks, columns, width = turned.shape
    total = jnp.zeros((columns, width), jnp.float32)
    for k in kinds:
        first = (block + blocks - offsets[k]) & (blocks - 1)
        second = (block + blocks - offsets[k + 1]) & (blocks - 1)
        left = jnp.concatenate([turned[first], turned[second]], axis=1)
        right = jnp.concatenate([tiles[first, k], tiles[second, k + 1]], axis=0)
        total += jnp.dot(left, right, preferred_element_type=jnp.float32)
    return total


def backward_rows(start, kinds, offsets, tiles, squares, turned, given, out):
    blocks, columns, width = turned.shape
    columns = columns // 2
    each = blocks // 2
    code = code_of(squares[...], blocks * width)
    scale = jnp.exp2(code)
    for part in range(2):
        out[part, each * width :] = jnp.broadcast_to(code, (CODE_ROWS, columns))

        @pl.loop(0, each // ROWS_PER_STEP)
        def _(step):
            for local in range(ROWS_PER_STEP):
                at = step * ROWS_PER_STEP + local
                block = (start + part * each + at) & (blocks - 1)
                total = backward_block(block, kinds, offsets, tiles, turned)
                if given is not None:
                    total += given[block]
                result = (total[:columns] + total[columns:]).T * scale
                out[part, pl.ds(pl.multiple_of(at * width, width), width)] = result


def backward_loading_kernel(offsets, half, source, near, out, tiles, squares, turned, given, arrived):
    blocks = near.shape[0]
    steps = arrived.shape[0]
    each = tiles.shape[1] // steps

    def load(step):
        part = pl.ds(step * each, each)
        return pltpu.make_async_copy(source.at[:, part], tiles.at[:, part], arrived.at[step])

    for step in range(steps):
        load(step).start()
    squares[...] = jnp.zeros_like(squares)
    for block in range(blocks):
        turn_rows(block, near[block], squares, turned)
    for step in range(steps):
        load(step).wait()
        kinds = range(step * each, (step + 1) * each, 2)
        if step == steps - 1:
            backward_rows(
                half[0] * (blocks // 2), kinds, offsets, tiles, squares, turned, given, out
            )
            continue

        @pl.loop(0, blocks // ROWS_PER_STEP)
        def _(at):
            for local in range(ROWS_PER_STEP):
                block = at * ROWS_PER_STEP + local
                total = backward_block(block, kinds, offsets, tiles, turned)
                given[block] = total if step == 0 else given[block] + total


def backward_kernel(offsets, half, tiles, own_half, other_half, out, squares, turned):
    each = own_half.shape[0]
    start = half[0] * each
    squares[...] = jnp.zeros_like(squares)
    for block in range(each):
        turn_rows(start + block, own_half[block], squares, turned)
        turn_rows(each - start + block, other_half[block], squares, turned)
    kinds = range(0, tiles.shape[1], 2)
    backward_rows(start, kinds, offsets, tiles, squares, turned, None, out)


def gram_kernel(start, first, second, out):
    count, width, columns = start.shape

    def total(function):
        sums = jnp.zeros((width, columns), jnp.float32)
        for block in range(count):
            sums += function(start[block], first[block], second[block])
        return jnp.sum(sums, axis=0, keepdims=True)

    weight = total(lambda s, u, v: s * s)
    usable = weight > 0
    safe = jnp.where(usable, weight, 1.0)
    a = jnp.where(usable, total(lambda s, u, v: s * u) / safe, 0.0)
    b = jnp.where(usable, total(lambda s, u, v: s * (v - a * u)) / safe, 0.0)
    uu = total(lambda s, u, v: (u - a * s) * (u - a * s))
    uv = total(lambda s, u, v: (u - a * s) * (v - a * u - b * s))
    vv = total(lambda s, u, v: (v - a * u - b * s) * (v - a * u - b * s))
    values = jnp.concatenate([a, b, weight, uu, uv, vv, uu, uu], axis=0)
    for copy in range(out.shape[0]):
        out[copy] = values


def last_kernel(count, half, found, start, first_own, first_other, second_own, second_other, coefficients, out):
    a, b, weight, uu, uv, vv = (found[:, k, :] for k in range(6))

    def mean(value):
        return jnp.sum(value, axis=0, keepdims=True) * (1.0 / count)

    norm = jnp.sqrt(mean(weight) + EPS)
    inverse = 1.0 / norm
    alpha_one = mean(a * weight) * inverse * inverse
    delta = a - alpha_one
    beta_one = jnp.sqrt(mean(uu + delta * delta * weight) * inverse * inverse + EPS)
    k = inverse / beta_one
    shift = b + delta * a - beta_one * beta_one
    alpha_two = k * k * mean(uv + delta * uu + delta * shift * weight)
    along = delta - alpha_two
    rest = shift - alpha_two * delta
    square = mean(vv + 2.0 * along * uv + along * along * uu + rest * rest * weight)
    beta_two = jnp.sqrt(k * k * square + EPS)
    coefficients[0:1] = alpha_one
    coefficients[1:2] = alpha_two
    coefficients[2:3] = beta_one
    coefficients[3:4] = beta_two
    of_start = (k * alpha_one * alpha_two - beta_one * inverse) / beta_two
    of_first = -k * (alpha_one + alpha_two) / beta_two
    of_second = k / beta_two
    each = first_own.shape[0]
    begin = half[0] * each
    for first, second, base in (
        (first_own, second_own, begin),
        (first_other, second_other, each - begin),
    ):
        for block in range(each):
            out[base + block] = (
                of_start * start[base + block] + of_first * first[block] + of_second * second[block]
            )


def small_call(kernel, name, out_shape, *values, first=None):
    specs = [whole_vmem()] * len(values)
    if first is not None:
        specs = [whole_smem()] + specs
        values = (first,) + values
    return pl.pallas_call(
        kernel,
        out_shape=out_shape,
        in_specs=specs,
        out_specs=tuple(whole_vmem() for _ in out_shape),
        compiler_params=pltpu.CompilerParams(vmem_limit_bytes=VMEM_LIMIT),
        cost_estimate=pl.CostEstimate(flops=0, bytes_accessed=2**16, transcendentals=0),
        name=name,
    )(*values)


def call(kernel, name, out_shape, scratch, offsets, half, tiles, *values):
    loading = kernel is backward_loading_kernel
    beside = kernel is forward_second_kernel
    return pl.pallas_call(
        kernel,
        out_shape=out_shape,
        in_specs=[whole_smem(), whole_smem(), pl.BlockSpec(memory_space=pl.ANY) if loading else whole_vmem()]
        + [whole_vmem()] * len(values),
        out_specs=tuple(whole_vmem() for _ in out_shape),
        scratch_shapes=scratch,
        compiler_params=pltpu.CompilerParams(
            vmem_limit_bytes=LOADING_VMEM_LIMIT if loading else VMEM_LIMIT
        ),
        cost_estimate=pl.CostEstimate(
            flops=2**30 if beside else 0,
            bytes_accessed=2**20 if beside else 2**16,
            transcendentals=0,
        ),
        name=name,
    )(offsets, half, tiles, *values)


def forward_product(tiles, offsets, half, own_half, other_half):
    blocks, _, width, _ = tiles.shape
    columns = own_half.shape[-1]
    each = blocks // 2
    shape = (each, width, columns)
    message = jax.ShapeDtypeStruct((each * width + CODE_ROWS, columns), jnp.float32)
    part = jax.ShapeDtypeStruct((each * width, columns), jnp.float32)
    other, halves = call(
        forward_first_kernel,
        "forward_first",
        (message, pltpu.VMEM((blocks, width, 2 * columns), jnp.bfloat16)),
        [],
        offsets, half, tiles, own_half.reshape(shape), other_half.reshape(shape),
    )
    (own,) = call(forward_second_kernel, "forward_second", (part,), [], offsets, half, tiles, halves)
    return other, own


def messages_shape(blocks, width, columns):
    return (2, blocks // 2 * width + CODE_ROWS, columns)


def backward_scratch(blocks, width, columns):
    return [
        pltpu.VMEM((1, columns), jnp.float32),
        pltpu.VMEM((blocks, 2 * columns, width), jnp.bfloat16),
    ]


def backward_loading(tiles, offsets, half, near):
    blocks, _, width, _ = tiles.shape
    columns = near.shape[-1]
    out, kept = call(
        backward_loading_kernel,
        "backward_loading",
        (
            pltpu.VMEM(messages_shape(blocks, width, columns), jnp.float32),
            pltpu.VMEM(tiles.shape, tiles.dtype),
        ),
        backward_scratch(blocks, width, columns)
        + [pltpu.VMEM((blocks, 2 * columns, width), jnp.float32), pltpu.SemaphoreType.DMA((3,))],
        offsets, half, tiles, near.reshape(blocks, width, columns),
    )
    return (out[0].astype(WIRE), out[1].astype(WIRE)), kept


def backward_product(tiles, offsets, half, own_half, other_half):
    blocks, _, width, _ = tiles.shape
    columns = own_half.shape[-1]
    shape = (blocks // 2, width, columns)
    (out,) = call(
        backward_kernel,
        "backward",
        (jax.ShapeDtypeStruct(messages_shape(blocks, width, columns), jnp.float32),),
        backward_scratch(blocks, width, columns),
        offsets, half, tiles, own_half.reshape(shape), other_half.reshape(shape),
    )
    return out[0].astype(WIRE), out[1].astype(WIRE)


AXES = ("row", "half", "line")


def permute(value, place):
    rows = lax.axis_size("row")
    cols = lax.axis_size("half") * lax.axis_size("line")
    pairs = []
    for r in range(rows):
        for c in range(cols):
            to_row, to_col = place(r, c, c ^ (cols // 2))
            pairs.append((r * cols + c, to_row % rows * cols + to_col))
    return lax.ppermute(value, AXES, pairs)


def swap(value):
    return permute(value, lambda r, c, o: (r, o))


def fetch(value):
    own = permute(value, lambda r, c, o: (r - c, c))
    return own, permute(value, lambda r, c, o: (r - o, o))


def give_back(own, other):
    same = permute(own, lambda r, c, o: (r + c, c))
    return same, permute(other, lambda r, c, o: (r + c, o))


def pack(value, code):
    codes = jnp.broadcast_to(code, value.shape[:-2] + (CODE_ROWS, value.shape[-1]))
    return jnp.concatenate([(value * jnp.exp2(code)).astype(WIRE), codes.astype(WIRE)], axis=-2)


def code_in(message):
    rows = message.shape[-2] - CODE_ROWS
    return message[..., rows : rows + 1, :].astype(jnp.float32)


def decode(message):
    rows = message.shape[-2] - CODE_ROWS
    return message[..., :rows, :].astype(jnp.float32) * jnp.exp2(-code_in(message))


def encode(value):
    peak = jnp.max(jnp.abs(value), axis=-2, keepdims=True)
    return pack(value, PEAK_EXPONENT - jnp.floor(jnp.log2(jnp.maximum(peak, TINY))))


def sum_line(partial, code):
    count = lax.axis_size("line")
    rows, columns = partial.shape
    parts = pack(partial.reshape(count, rows // count, columns), code)
    parts = lax.all_to_all(parts, "line", 0, 0)
    code = jnp.min(code_in(parts), axis=0) - (count - 1).bit_length()
    share = pack(jnp.sum(decode(parts), axis=0), code)
    return lax.all_to_all(jnp.broadcast_to(share[None], parts.shape), "line", 0, 0)


def body(start_block, tiles, band_offsets):
    half = lax.axis_index("half")
    rows, height, columns = lax.axis_size("row"), *start_block.shape
    parts = lax.axis_size("line")
    blocks = tiles.shape[2]
    offsets = band_offsets[0, 0]
    place = half[None].astype(jnp.int32)
    start_half = lax.dynamic_slice_in_dim(start_block, half * (height // 2), height // 2, 0)
    start_half = start_half.reshape(parts, height // 2 // parts, columns)

    def apply(kept, far, back):
        other, own = forward_product(kept, offsets, place, decode(far[0]), decode(far[1]))
        given = swap(other.astype(WIRE))
        own, *back = lax.optimization_barrier((own, *back))
        arrived = own + decode(back[0]) + decode(back[1])
        code = jnp.minimum(code_in(other), code_in(given))
        code = jnp.minimum(code, jnp.minimum(code_in(back[0]), code_in(back[1]))) - 2.0
        return sum_line(arrived + decode(given), code)

    far = fetch(encode(start_half))
    back, kept = backward_loading(tiles[0, 0], offsets, place, start_block)
    first = apply(kept, far, give_back(*back))

    first_other = swap(first)
    far = fetch(first)
    first, first_other = decode(first), decode(first_other)
    back = backward_product(kept, offsets, place, first, first_other)
    second = apply(kept, far, give_back(*back))

    second_other = swap(second)
    second = decode(second)
    (found,) = small_call(
        gram_kernel,
        "gram",
        (jax.ShapeDtypeStruct((2 * rows, 8, columns), jnp.float32),),
        start_half, first, second,
    )
    found = lax.all_to_all(found, ("row", "half"), 0, 0)
    found, second_other = lax.optimization_barrier((found, second_other))
    in_blocks = [
        value.reshape(-1, height // blocks, columns)
        for value in (start_block, first, first_other, second, decode(second_other))
    ]
    coefficients, q_third = small_call(
        functools.partial(last_kernel, height * rows),
        "last",
        (
            jax.ShapeDtypeStruct((4, columns), jnp.float32),
            jax.ShapeDtypeStruct((blocks, height // blocks, columns), jnp.float32),
        ),
        found, *in_blocks, first=place,
    )
    return (coefficients[0:2], coefficients[2:4], q_third.reshape(height, columns))


def solution(mesh):
    rows, cols = mesh.devices.shape
    parted = jax.sharding.Mesh(mesh.devices.reshape(rows, 2, cols // 2), AXES)
    split = ("half", "line")
    placed = (P("row", None), P("row", split, None, None, None, None), P("row", split, None))
    return jax.shard_map(
        body, mesh=parted, in_specs=placed, out_specs=(P(), P(), P("row", None)), check_vma=False
    )
```

```python
import functools

import jax
import jax.numpy as jnp
from jax import lax
from jax.experimental import pallas as pl
from jax.experimental.pallas import tpu as pltpu
from jax.sharding import PartitionSpec as P

EPS = 1e-06
TINY = 1e-30
WIRE = jnp.float16
SEGMENT_SCALE = 1024.0
CODE_ROWS = 8
ROWS_PER_STEP = 8
VMEM_LIMIT = 24 * 2**20
LOADING_VMEM_LIMIT = 53 * 2**20


def whole_vmem():
    return pl.BlockSpec(memory_space=pltpu.VMEM)


def whole_smem():
    return pl.BlockSpec(memory_space=pltpu.SMEM)


def low_part(value, high):
    return (value - high.astype(jnp.float32)).astype(jnp.bfloat16)


def code_of(squares, rows):
    return jnp.floor(jnp.log2(SEGMENT_SCALE * lax.rsqrt(squares * (1.0 / rows) + TINY)))


def merged(total, columns, axis):
    if total.shape[axis] == columns:
        return total
    return sum(jnp.split(total, 2, axis=axis))


def forward_rows(begin, offsets, tiles, halves, out, factor):
    blocks, width = halves.shape[:2]
    kept = tiles.shape[1]

    @pl.loop(0, blocks // 2 // ROWS_PER_STEP)
    def _(step):
        for local in range(ROWS_PER_STEP):
            at = step * ROWS_PER_STEP + local
            row = begin + at
            total = jnp.zeros((width, halves.shape[2]), jnp.float32)
            for k in range(0, kept, 2):
                first = halves[(row + offsets[k]) & (blocks - 1)]
                second = halves[(row + offsets[k + 1]) & (blocks - 1)]
                left = jnp.concatenate([tiles[row, k], tiles[row, k + 1]], axis=1)
                right = jnp.concatenate([first, second], axis=0)
                total += jnp.dot(left, right, preferred_element_type=jnp.float32)
            result = merged(total, out.shape[1], 1)
            out[pl.ds(pl.multiple_of(at * width, width), width)] = (
                result if factor is None else result * factor
            )


def forward_start_kernel(offsets, half, tiles, far, out):
    blocks, width, columns = far.shape
    squares = jnp.zeros((1, columns), jnp.float32)
    for block in range(blocks):
        value = far[block].astype(jnp.float32)
        squares += jnp.sum(value * value, axis=0, keepdims=True)
    code = code_of(squares, blocks * width)
    out[blocks // 2 * width :] = jnp.broadcast_to(code, (CODE_ROWS, columns))
    begin = (1 - half[0]) * (blocks // 2)
    forward_rows(begin, offsets, tiles, far, out, jnp.exp2(code))


def forward_first_kernel(offsets, half, tiles, own_half, other_half, out, halves):
    each, width, columns = own_half.shape
    start = half[0] * each
    squares = jnp.zeros((1, columns), jnp.float32)
    for block in range(each):
        for source, base in ((own_half, start), (other_half, each - start)):
            value = source[block]
            squares += jnp.sum(value * value, axis=0, keepdims=True)
            high = value.astype(jnp.bfloat16)
            halves[base + block] = jnp.concatenate([high, low_part(value, high)], axis=1)
    code = code_of(squares, 2 * each * width)
    out[each * width :] = jnp.broadcast_to(code, (CODE_ROWS, columns))
    forward_rows(each - start, offsets, tiles, halves, out, jnp.exp2(code))


def forward_second_kernel(offsets, half, tiles, halves, out):
    forward_rows(half[0] * (halves.shape[0] // 2), offsets, tiles, halves, out, None)


def turn_rows(block, value, squares, turned):
    squares[...] += jnp.sum(value * value, axis=0, keepdims=True)
    value = value.T
    high = value.astype(jnp.bfloat16)
    if turned.shape[1] == high.shape[0]:
        turned[block] = high
    else:
        turned[block] = jnp.concatenate([high, low_part(value, high)], axis=0)


def backward_block(block, kinds, offsets, tiles, turned):
    blocks, columns, width = turned.shape
    total = jnp.zeros((columns, width), jnp.float32)
    for k in kinds:
        first = (block + blocks - offsets[k]) & (blocks - 1)
        second = (block + blocks - offsets[k + 1]) & (blocks - 1)
        left = jnp.concatenate([turned[first], turned[second]], axis=1)
        right = jnp.concatenate([tiles[first, k], tiles[second, k + 1]], axis=0)
        total += jnp.dot(left, right, preferred_element_type=jnp.float32)
    return total


def backward_rows(start, kinds, offsets, tiles, squares, turned, given, out):
    blocks, _, width = turned.shape
    columns = squares.shape[1]
    each = blocks // 2
    code = code_of(squares[...], blocks * width)
    scale = jnp.exp2(code)
    for part in range(2):
        out[part, each * width :] = jnp.broadcast_to(code, (CODE_ROWS, columns))

        @pl.loop(0, each // ROWS_PER_STEP)
        def _(step):
            for local in range(ROWS_PER_STEP):
                at = step * ROWS_PER_STEP + local
                block = (start + part * each + at) & (blocks - 1)
                total = backward_block(block, kinds, offsets, tiles, turned)
                if given is not None:
                    total += given[block]
                result = merged(total, columns, 0).T * scale
                out[part, pl.ds(pl.multiple_of(at * width, width), width)] = result


def backward_loading_kernel(offsets, half, source, near, out, tiles, squares, turned, given, arrived):
    blocks = near.shape[0]
    steps = arrived.shape[0]
    each = tiles.shape[1] // steps

    def load(step):
        part = pl.ds(step * each, each)
        return pltpu.make_async_copy(source.at[:, part], tiles.at[:, part], arrived.at[step])

    for step in range(steps):
        load(step).start()
    squares[...] = jnp.zeros_like(squares)
    for block in range(blocks):
        turn_rows(block, near[block], squares, turned)
    for step in range(steps):
        load(step).wait()
        kinds = range(step * each, (step + 1) * each, 2)
        if step == steps - 1:
            backward_rows(
                half[0] * (blocks // 2), kinds, offsets, tiles, squares, turned, given, out
            )
            continue

        @pl.loop(0, blocks // ROWS_PER_STEP)
        def _(at):
            for local in range(ROWS_PER_STEP):
                block = at * ROWS_PER_STEP + local
                total = backward_block(block, kinds, offsets, tiles, turned)
                given[block] = total if step == 0 else given[block] + total


def backward_kernel(offsets, half, tiles, own_half, other_half, out, squares, turned):
    each = own_half.shape[0]
    start = half[0] * each
    squares[...] = jnp.zeros_like(squares)
    for block in range(each):
        turn_rows(start + block, own_half[block], squares, turned)
        turn_rows(each - start + block, other_half[block], squares, turned)
    kinds = range(0, tiles.shape[1], 2)
    backward_rows(start, kinds, offsets, tiles, squares, turned, None, out)


def gram_kernel(start, first, second, out):
    count, width, columns = start.shape

    def total(function):
        sums = jnp.zeros((width, columns), jnp.float32)
        for block in range(count):
            sums += function(start[block], first[block], second[block])
        return jnp.sum(sums, axis=0, keepdims=True)

    weight = total(lambda s, u, v: s * s)
    usable = weight > 0
    safe = jnp.where(usable, weight, 1.0)
    a = jnp.where(usable, total(lambda s, u, v: s * u) / safe, 0.0)
    b = jnp.where(usable, total(lambda s, u, v: s * (v - a * u)) / safe, 0.0)
    uu = total(lambda s, u, v: (u - a * s) * (u - a * s))
    uv = total(lambda s, u, v: (u - a * s) * (v - a * u - b * s))
    vv = total(lambda s, u, v: (v - a * u - b * s) * (v - a * u - b * s))
    values = jnp.concatenate([a, b, weight, uu, uv, vv, uu, uu], axis=0)
    for copy in range(out.shape[0]):
        out[copy] = values


def last_kernel(count, half, found, start, first_own, first_other, second_own, second_other, alphas, betas, out):
    a, b, weight, uu, uv, vv = (found[:, k, :] for k in range(6))

    def mean(value):
        return jnp.sum(value, axis=0, keepdims=True) * (1.0 / count)

    norm = jnp.sqrt(mean(weight) + EPS)
    inverse = 1.0 / norm
    alpha_one = mean(a * weight) * inverse * inverse
    delta = a - alpha_one
    beta_one = jnp.sqrt(mean(uu + delta * delta * weight) * inverse * inverse + EPS)
    k = inverse / beta_one
    shift = b + delta * a - beta_one * beta_one
    alpha_two = k * k * mean(uv + delta * uu + delta * shift * weight)
    along = delta - alpha_two
    rest = shift - alpha_two * delta
    square = mean(vv + 2.0 * along * uv + along * along * uu + rest * rest * weight)
    beta_two = jnp.sqrt(k * k * square + EPS)
    alphas[...] = jnp.concatenate([alpha_one, alpha_two], axis=0)
    betas[...] = jnp.concatenate([beta_one, beta_two], axis=0)
    of_start = (k * alpha_one * alpha_two - beta_one * inverse) / beta_two
    of_first = -k * (alpha_one + alpha_two) / beta_two
    of_second = k / beta_two
    each = first_own.shape[0]
    begin = half[0] * each
    for first, second, base in (
        (first_own, second_own, begin),
        (first_other, second_other, each - begin),
    ):
        for block in range(each):
            out[base + block] = (
                of_start * start[base + block] + of_first * first[block] + of_second * second[block]
            )


def small_call(kernel, name, out_shape, *values, first=None):
    specs = [whole_vmem()] * len(values)
    if first is not None:
        specs = [whole_smem()] + specs
        values = (first,) + values
    return pl.pallas_call(
        kernel,
        out_shape=out_shape,
        in_specs=specs,
        out_specs=tuple(whole_vmem() for _ in out_shape),
        compiler_params=pltpu.CompilerParams(vmem_limit_bytes=VMEM_LIMIT),
        cost_estimate=pl.CostEstimate(flops=0, bytes_accessed=2**16, transcendentals=0),
        name=name,
    )(*values)


def call(kernel, name, out_shape, scratch, offsets, half, tiles, *values):
    loading = kernel is backward_loading_kernel
    beside = kernel is forward_second_kernel
    return pl.pallas_call(
        kernel,
        out_shape=out_shape,
        in_specs=[whole_smem(), whole_smem(), pl.BlockSpec(memory_space=pl.ANY) if loading else whole_vmem()]
        + [whole_vmem()] * len(values),
        out_specs=tuple(whole_vmem() for _ in out_shape),
        scratch_shapes=scratch,
        compiler_params=pltpu.CompilerParams(
            vmem_limit_bytes=LOADING_VMEM_LIMIT if loading else VMEM_LIMIT
        ),
        cost_estimate=pl.CostEstimate(
            flops=2**30 if beside else 0,
            bytes_accessed=2**20 if beside else 2**16,
            transcendentals=0,
        ),
        name=name,
    )(offsets, half, tiles, *values)


def forward_product(tiles, offsets, half, far):
    blocks, _, width, _ = tiles.shape
    columns = far[0].shape[-1]
    each = blocks // 2
    message = jax.ShapeDtypeStruct((each * width + CODE_ROWS, columns), jnp.float32)
    part = jax.ShapeDtypeStruct((each * width, columns), jnp.float32)
    if len(far) == 1:
        halves = far[0].reshape(blocks, width, columns)
        (other,) = call(
            forward_start_kernel, "forward_start", (message,), [], offsets, half, tiles, halves
        )
    else:
        other, halves = call(
            forward_first_kernel,
            "forward_first",
            (message, pltpu.VMEM((blocks, width, 2 * columns), jnp.bfloat16)),
            [],
            offsets, half, tiles, *(value.reshape(each, width, columns) for value in far),
        )
    (own,) = call(forward_second_kernel, "forward_second", (part,), [], offsets, half, tiles, halves)
    return other, own


def messages_shape(blocks, width, columns):
    return (2, blocks // 2 * width + CODE_ROWS, columns)


def backward_scratch(blocks, width, columns, halves):
    return [
        pltpu.VMEM((1, columns), jnp.float32),
        pltpu.VMEM((blocks, halves * columns, width), jnp.bfloat16),
    ]


def backward_loading(tiles, offsets, half, near):
    blocks, _, width, _ = tiles.shape
    columns = near.shape[-1]
    out, kept = call(
        backward_loading_kernel,
        "backward_loading",
        (
            pltpu.VMEM(messages_shape(blocks, width, columns), jnp.float32),
            pltpu.VMEM(tiles.shape, tiles.dtype),
        ),
        backward_scratch(blocks, width, columns, 1)
        + [pltpu.VMEM((blocks, columns, width), jnp.float32), pltpu.SemaphoreType.DMA((3,))],
        offsets, half, tiles, near.reshape(blocks, width, columns),
    )
    return (out[0].astype(WIRE), out[1].astype(WIRE)), kept


def backward_product(tiles, offsets, half, own_half, other_half):
    blocks, _, width, _ = tiles.shape
    columns = own_half.shape[-1]
    shape = (blocks // 2, width, columns)
    (out,) = call(
        backward_kernel,
        "backward",
        (jax.ShapeDtypeStruct(messages_shape(blocks, width, columns), jnp.float32),),
        backward_scratch(blocks, width, columns, 2),
        offsets, half, tiles, own_half.reshape(shape), other_half.reshape(shape),
    )
    return out[0].astype(WIRE), out[1].astype(WIRE)


AXES = ("row", "half", "line")


def permute(value, place):
    rows = lax.axis_size("row")
    cols = lax.axis_size("half") * lax.axis_size("line")
    pairs = []
    for r in range(rows):
        for c in range(cols):
            to_row, to_col = place(r, c, c ^ (cols // 2))
            pairs.append((r * cols + c, to_row % rows * cols + to_col))
    return lax.ppermute(value, AXES, pairs)


def swap(value):
    return permute(value, lambda r, c, o: (r, o))


def fetch(value):
    own = permute(value, lambda r, c, o: (r - c, c))
    return own, permute(value, lambda r, c, o: (r - o, o))


def fetch_whole(value):
    return permute(value, lambda r, c, o: (r - o, o))


def give_back(own, other):
    same = permute(own, lambda r, c, o: (r + c, c))
    return same, permute(other, lambda r, c, o: (r + c, o))


def pack(value, code):
    codes = jnp.broadcast_to(code, value.shape[:-2] + (CODE_ROWS, value.shape[-1]))
    return jnp.concatenate([(value * jnp.exp2(code)).astype(WIRE), codes.astype(WIRE)], axis=-2)


def code_in(message):
    rows = message.shape[-2] - CODE_ROWS
    return message[..., rows : rows + 1, :].astype(jnp.float32)


def decode(message):
    rows = message.shape[-2] - CODE_ROWS
    return message[..., :rows, :].astype(jnp.float32) * jnp.exp2(-code_in(message))


def sum_line(partial, code):
    count = lax.axis_size("line")
    rows, columns = partial.shape
    parts = pack(partial.reshape(count, rows // count, columns), code)
    parts = lax.all_to_all(parts, "line", 0, 0)
    code = jnp.min(code_in(parts), axis=0) - (count - 1).bit_length()
    share = pack(jnp.sum(decode(parts), axis=0), code)
    return lax.all_to_all(jnp.broadcast_to(share[None], parts.shape), "line", 0, 0)


def body(start_block, tiles, band_offsets):
    half = lax.axis_index("half")
    rows, height, columns = lax.axis_size("row"), *start_block.shape
    parts = lax.axis_size("line")
    blocks = tiles.shape[2]
    offsets = band_offsets[0, 0]
    place = half[None].astype(jnp.int32)
    start_half = lax.dynamic_slice_in_dim(start_block, half * (height // 2), height // 2, 0)
    start_half = start_half.reshape(parts, height // 2 // parts, columns)

    def apply(kept, far, back):
        other, own = forward_product(kept, offsets, place, far)
        given = swap(other.astype(WIRE))
        own, *back = lax.optimization_barrier((own, *back))
        arrived = own + decode(back[0]) + decode(back[1])
        code = jnp.minimum(code_in(other), code_in(given))
        code = jnp.minimum(code, jnp.minimum(code_in(back[0]), code_in(back[1]))) - 2.0
        return sum_line(arrived + decode(given), code)

    far = (fetch_whole(start_block.astype(jnp.bfloat16)),)
    back, kept = backward_loading(tiles[0, 0], offsets, place, start_block)
    first = apply(kept, far, give_back(*back))

    first_other = swap(first)
    far = tuple(decode(message) for message in fetch(first))
    first, first_other = decode(first), decode(first_other)
    back = backward_product(kept, offsets, place, first, first_other)
    second = apply(kept, far, give_back(*back))

    second_other = swap(second)
    second = decode(second)
    (found,) = small_call(
        gram_kernel,
        "gram",
        (jax.ShapeDtypeStruct((2 * rows, 8, columns), jnp.float32),),
        start_half, first, second,
    )
    found = lax.all_to_all(found, ("row", "half"), 0, 0)
    found, second_other = lax.optimization_barrier((found, second_other))
    in_blocks = [
        value.reshape(-1, height // blocks, columns)
        for value in (start_block, first, first_other, second, decode(second_other))
    ]
    alphas, betas, q_third = small_call(
        functools.partial(last_kernel, height * rows),
        "last",
        (
            jax.ShapeDtypeStruct((2, columns), jnp.float32),
            jax.ShapeDtypeStruct((2, columns), jnp.float32),
            jax.ShapeDtypeStruct((blocks, height // blocks, columns), jnp.float32),
        ),
        found, *in_blocks, first=place,
    )
    return (alphas, betas, q_third.reshape(height, columns))


def solution(mesh):
    rows, cols = mesh.devices.shape
    parted = jax.sharding.Mesh(mesh.devices.reshape(rows, 2, cols // 2), AXES)
    split = ("half", "line")
    placed = (P("row", None), P("row", split, None, None, None, None), P("row", split, None))
    return jax.shard_map(
        body, mesh=parted, in_specs=placed, out_specs=(P(), P(), P("row", None)), check_vma=False
    )
```

```python
import functools

import jax
import jax.numpy as jnp
from jax import lax
from jax.experimental import pallas as pl
from jax.experimental.pallas import tpu as pltpu
from jax.sharding import PartitionSpec as P

EPS = 1e-06
TINY = 1e-30
WIRE = jnp.float16
SEGMENT_SCALE = 1024.0
CODE_ROWS = 8
ROWS_PER_STEP = 8
VMEM_LIMIT = 24 * 2**20
LOADING_VMEM_LIMIT = 53 * 2**20


def whole_vmem():
    return pl.BlockSpec(memory_space=pltpu.VMEM)


def whole_smem():
    return pl.BlockSpec(memory_space=pltpu.SMEM)


def low_part(value, high):
    return (value - high.astype(jnp.float32)).astype(jnp.bfloat16)


def code_of(squares, rows):
    return jnp.floor(jnp.log2(SEGMENT_SCALE * lax.rsqrt(squares * (1.0 / rows) + TINY)))


def merged(total, columns, axis):
    if total.shape[axis] == columns:
        return total
    return sum(jnp.split(total, 2, axis=axis))


def forward_rows(begin, offsets, tiles, halves, out, factor):
    blocks, width = halves.shape[:2]
    kept = tiles.shape[1]

    @pl.loop(0, blocks // 2 // ROWS_PER_STEP)
    def _(step):
        for local in range(ROWS_PER_STEP):
            at = step * ROWS_PER_STEP + local
            row = begin + at
            total = jnp.zeros((width, halves.shape[2]), jnp.float32)
            for k in range(0, kept, 2):
                first = halves[(row + offsets[k]) & (blocks - 1)]
                second = halves[(row + offsets[k + 1]) & (blocks - 1)]
                left = jnp.concatenate([tiles[row, k], tiles[row, k + 1]], axis=1)
                right = jnp.concatenate([first, second], axis=0)
                total += jnp.dot(left, right, preferred_element_type=jnp.float32)
            result = merged(total, out.shape[1], 1)
            out[pl.ds(pl.multiple_of(at * width, width), width)] = (
                result if factor is None else result * factor
            )


def forward_start_kernel(offsets, half, tiles, far, out):
    blocks, width, columns = far.shape
    squares = jnp.zeros((1, columns), jnp.float32)
    for block in range(blocks):
        value = far[block].astype(jnp.float32)
        squares += jnp.sum(value * value, axis=0, keepdims=True)
    code = code_of(squares, blocks * width)
    out[blocks // 2 * width :] = jnp.broadcast_to(code, (CODE_ROWS, columns))
    begin = (1 - half[0]) * (blocks // 2)
    forward_rows(begin, offsets, tiles, far, out, jnp.exp2(code))


def forward_first_kernel(offsets, half, tiles, own_half, other_half, out, halves):
    each, width, columns = own_half.shape
    start = half[0] * each
    squares = jnp.zeros((1, columns), jnp.float32)
    for block in range(each):
        for source, base in ((own_half, start), (other_half, each - start)):
            value = source[block]
            squares += jnp.sum(value * value, axis=0, keepdims=True)
            high = value.astype(jnp.bfloat16)
            halves[base + block] = jnp.concatenate([high, low_part(value, high)], axis=1)
    code = code_of(squares, 2 * each * width)
    out[each * width :] = jnp.broadcast_to(code, (CODE_ROWS, columns))
    forward_rows(each - start, offsets, tiles, halves, out, jnp.exp2(code))


def forward_second_kernel(offsets, half, tiles, halves, out):
    forward_rows(half[0] * (halves.shape[0] // 2), offsets, tiles, halves, out, None)


def turn_rows(block, value, squares, turned):
    squares[...] += jnp.sum(value * value, axis=0, keepdims=True)
    value = value.T
    high = value.astype(jnp.bfloat16)
    if turned.shape[1] == high.shape[0]:
        turned[block] = high
    else:
        turned[block] = jnp.concatenate([high, low_part(value, high)], axis=0)


def backward_block(block, kinds, offsets, tiles, turned):
    blocks, columns, width = turned.shape
    total = jnp.zeros((columns, width), jnp.float32)
    for k in kinds:
        first = (block + blocks - offsets[k]) & (blocks - 1)
        second = (block + blocks - offsets[k + 1]) & (blocks - 1)
        left = jnp.concatenate([turned[first], turned[second]], axis=1)
        right = jnp.concatenate([tiles[first, k], tiles[second, k + 1]], axis=0)
        total += jnp.dot(left, right, preferred_element_type=jnp.float32)
    return total


def backward_rows(start, kinds, offsets, tiles, squares, turned, given, out):
    blocks, _, width = turned.shape
    columns = squares.shape[1]
    each = blocks // 2
    code = code_of(squares[...], blocks * width)
    scale = jnp.exp2(code)
    for part in range(2):
        out[part, each * width :] = jnp.broadcast_to(code, (CODE_ROWS, columns))

        @pl.loop(0, each // ROWS_PER_STEP)
        def _(step):
            for local in range(ROWS_PER_STEP):
                at = step * ROWS_PER_STEP + local
                block = (start + part * each + at) & (blocks - 1)
                total = backward_block(block, kinds, offsets, tiles, turned)
                if given is not None:
                    total += given[block]
                result = merged(total, columns, 0).T * scale
                out[part, pl.ds(pl.multiple_of(at * width, width), width)] = result


def backward_loading_kernel(offsets, half, source, near, out, tiles, squares, turned, given, arrived):
    blocks = near.shape[0]
    steps = arrived.shape[0]
    each = tiles.shape[1] // steps

    def load(step):
        part = pl.ds(step * each, each)
        return pltpu.make_async_copy(source.at[:, part], tiles.at[:, part], arrived.at[step])

    for step in range(steps):
        load(step).start()
    squares[...] = jnp.zeros_like(squares)
    for block in range(blocks):
        turn_rows(block, near[block].astype(jnp.float32), squares, turned)
    for step in range(steps):
        load(step).wait()
        kinds = range(step * each, (step + 1) * each, 2)
        if step == steps - 1:
            backward_rows(
                half[0] * (blocks // 2), kinds, offsets, tiles, squares, turned, given, out
            )
            continue

        @pl.loop(0, blocks // ROWS_PER_STEP)
        def _(at):
            for local in range(ROWS_PER_STEP):
                block = at * ROWS_PER_STEP + local
                total = backward_block(block, kinds, offsets, tiles, turned)
                given[block] = total if step == 0 else given[block] + total


def backward_kernel(offsets, half, tiles, own_half, other_half, out, squares, turned):
    each = own_half.shape[0]
    start = half[0] * each
    squares[...] = jnp.zeros_like(squares)
    for block in range(each):
        turn_rows(start + block, own_half[block], squares, turned)
        turn_rows(each - start + block, other_half[block], squares, turned)
    kinds = range(0, tiles.shape[1], 2)
    backward_rows(start, kinds, offsets, tiles, squares, turned, None, out)


def gram_kernel(half, start, first, second, out):
    count, width, columns = first.shape
    begin = half[0] * count

    def total(function):
        sums = jnp.zeros((width, columns), jnp.float32)
        for block in range(count):
            sums += function(start[begin + block], first[block], second[block])
        return jnp.sum(sums, axis=0, keepdims=True)

    weight = total(lambda s, u, v: s * s)
    usable = weight > 0
    safe = jnp.where(usable, weight, 1.0)
    a = jnp.where(usable, total(lambda s, u, v: s * u) / safe, 0.0)
    b = jnp.where(usable, total(lambda s, u, v: s * (v - a * u)) / safe, 0.0)
    uu = total(lambda s, u, v: (u - a * s) * (u - a * s))
    uv = total(lambda s, u, v: (u - a * s) * (v - a * u - b * s))
    vv = total(lambda s, u, v: (v - a * u - b * s) * (v - a * u - b * s))
    values = jnp.concatenate([a, b, weight, uu, uv, vv, uu, uu], axis=0)
    for copy in range(out.shape[0]):
        out[copy] = values


def last_kernel(count, half, found, start, first_own, first_other, second_own, second_other, alphas, betas, out):
    a, b, weight, uu, uv, vv = (found[:, k, :] for k in range(6))

    def mean(value):
        return jnp.sum(value, axis=0, keepdims=True) * (1.0 / count)

    norm = jnp.sqrt(mean(weight) + EPS)
    inverse = 1.0 / norm
    alpha_one = mean(a * weight) * inverse * inverse
    delta = a - alpha_one
    beta_one = jnp.sqrt(mean(uu + delta * delta * weight) * inverse * inverse + EPS)
    k = inverse / beta_one
    shift = b + delta * a - beta_one * beta_one
    alpha_two = k * k * mean(uv + delta * uu + delta * shift * weight)
    along = delta - alpha_two
    rest = shift - alpha_two * delta
    square = mean(vv + 2.0 * along * uv + along * along * uu + rest * rest * weight)
    beta_two = jnp.sqrt(k * k * square + EPS)
    alphas[...] = jnp.concatenate([alpha_one, alpha_two], axis=0)
    betas[...] = jnp.concatenate([beta_one, beta_two], axis=0)
    of_start = (k * alpha_one * alpha_two - beta_one * inverse) / beta_two
    of_first = -k * (alpha_one + alpha_two) / beta_two
    of_second = k / beta_two
    each = first_own.shape[0]
    begin = half[0] * each
    for first, second, base in (
        (first_own, second_own, begin),
        (first_other, second_other, each - begin),
    ):
        for block in range(each):
            out[base + block] = (
                of_start * start[base + block] + of_first * first[block] + of_second * second[block]
            )


def small_call(kernel, name, out_shape, *values, first=None):
    specs = [whole_vmem()] * len(values)
    if first is not None:
        specs = [whole_smem()] + specs
        values = (first,) + values
    return pl.pallas_call(
        kernel,
        out_shape=out_shape,
        in_specs=specs,
        out_specs=tuple(whole_vmem() for _ in out_shape),
        compiler_params=pltpu.CompilerParams(vmem_limit_bytes=VMEM_LIMIT),
        cost_estimate=pl.CostEstimate(flops=0, bytes_accessed=2**16, transcendentals=0),
        name=name,
    )(*values)


def call(kernel, name, out_shape, scratch, offsets, half, tiles, *values):
    loading = kernel is backward_loading_kernel
    beside = kernel is forward_second_kernel
    return pl.pallas_call(
        kernel,
        out_shape=out_shape,
        in_specs=[whole_smem(), whole_smem(), pl.BlockSpec(memory_space=pl.ANY) if loading else whole_vmem()]
        + [whole_vmem()] * len(values),
        out_specs=tuple(whole_vmem() for _ in out_shape),
        scratch_shapes=scratch,
        compiler_params=pltpu.CompilerParams(
            vmem_limit_bytes=LOADING_VMEM_LIMIT if loading else VMEM_LIMIT
        ),
        cost_estimate=pl.CostEstimate(
            flops=2**30 if beside else 0,
            bytes_accessed=2**20 if beside else 2**16,
            transcendentals=0,
        ),
        name=name,
    )(offsets, half, tiles, *values)


def forward_product(tiles, offsets, half, far):
    blocks, _, width, _ = tiles.shape
    columns = far[0].shape[-1]
    each = blocks // 2
    message = jax.ShapeDtypeStruct((each * width + CODE_ROWS, columns), jnp.float32)
    part = jax.ShapeDtypeStruct((each * width, columns), jnp.float32)
    if len(far) == 1:
        halves = far[0].reshape(blocks, width, columns)
        (other,) = call(
            forward_start_kernel, "forward_start", (message,), [], offsets, half, tiles, halves
        )
    else:
        other, halves = call(
            forward_first_kernel,
            "forward_first",
            (message, pltpu.VMEM((blocks, width, 2 * columns), jnp.bfloat16)),
            [],
            offsets, half, tiles, *(value.reshape(each, width, columns) for value in far),
        )
    (own,) = call(forward_second_kernel, "forward_second", (part,), [], offsets, half, tiles, halves)
    return other, own


def messages_shape(blocks, width, columns):
    return (2, blocks // 2 * width + CODE_ROWS, columns)


def backward_scratch(blocks, width, columns, halves):
    return [
        pltpu.VMEM((1, columns), jnp.float32),
        pltpu.VMEM((blocks, halves * columns, width), jnp.bfloat16),
    ]


def backward_loading(tiles, offsets, half, near):
    blocks, _, width, _ = tiles.shape
    columns = near.shape[-1]
    out, kept = call(
        backward_loading_kernel,
        "backward_loading",
        (
            pltpu.VMEM(messages_shape(blocks, width, columns), jnp.float32),
            pltpu.VMEM(tiles.shape, tiles.dtype),
        ),
        backward_scratch(blocks, width, columns, 1)
        + [pltpu.VMEM((blocks, columns, width), jnp.float32), pltpu.SemaphoreType.DMA((3,))],
        offsets, half, tiles, near.reshape(blocks, width, columns),
    )
    return (out[0].astype(WIRE), out[1].astype(WIRE)), kept


def backward_product(tiles, offsets, half, own_half, other_half):
    blocks, _, width, _ = tiles.shape
    columns = own_half.shape[-1]
    shape = (blocks // 2, width, columns)
    (out,) = call(
        backward_kernel,
        "backward",
        (jax.ShapeDtypeStruct(messages_shape(blocks, width, columns), jnp.float32),),
        backward_scratch(blocks, width, columns, 2),
        offsets, half, tiles, own_half.reshape(shape), other_half.reshape(shape),
    )
    return out[0].astype(WIRE), out[1].astype(WIRE)


AXES = ("row", "half", "line")


def permute(value, place):
    rows = lax.axis_size("row")
    cols = lax.axis_size("half") * lax.axis_size("line")
    pairs = []
    for r in range(rows):
        for c in range(cols):
            to_row, to_col = place(r, c, c ^ (cols // 2))
            pairs.append((r * cols + c, to_row % rows * cols + to_col))
    return lax.ppermute(value, AXES, pairs)


def swap(value):
    return permute(value, lambda r, c, o: (r, o))


def fetch(value):
    own = permute(value, lambda r, c, o: (r - c, c))
    return own, permute(value, lambda r, c, o: (r - o, o))


def fetch_whole(value):
    return permute(value, lambda r, c, o: (r - o, o))


def give_back(own, other):
    same = permute(own, lambda r, c, o: (r + c, c))
    return same, permute(other, lambda r, c, o: (r + c, o))


def pack(value, code):
    codes = jnp.broadcast_to(code, value.shape[:-2] + (CODE_ROWS, value.shape[-1]))
    return jnp.concatenate([(value * jnp.exp2(code)).astype(WIRE), codes.astype(WIRE)], axis=-2)


def code_in(message):
    rows = message.shape[-2] - CODE_ROWS
    return message[..., rows : rows + 1, :].astype(jnp.float32)


def decode(message):
    rows = message.shape[-2] - CODE_ROWS
    return message[..., :rows, :].astype(jnp.float32) * jnp.exp2(-code_in(message))


def sum_line(partial, code):
    count = lax.axis_size("line")
    rows, columns = partial.shape
    parts = pack(partial.reshape(count, rows // count, columns), code)
    parts = lax.all_to_all(parts, "line", 0, 0)
    code = jnp.min(code_in(parts), axis=0) - (count - 1).bit_length()
    share = pack(jnp.sum(decode(parts), axis=0), code)
    return lax.all_to_all(jnp.broadcast_to(share[None], parts.shape), "line", 0, 0)


def body(start_block, tiles, band_offsets):
    half = lax.axis_index("half")
    rows, height, columns = lax.axis_size("row"), *start_block.shape
    parts = lax.axis_size("line")
    blocks = tiles.shape[2]
    offsets = band_offsets[0, 0]
    place = half[None].astype(jnp.int32)
    def apply(kept, far, back):
        other, own = forward_product(kept, offsets, place, far)
        given = swap(other.astype(WIRE))
        own, *back = lax.optimization_barrier((own, *back))
        arrived = own + decode(back[0]) + decode(back[1])
        code = jnp.minimum(code_in(other), code_in(given))
        code = jnp.minimum(code, jnp.minimum(code_in(back[0]), code_in(back[1]))) - 2.0
        return sum_line(arrived + decode(given), code)

    rounded = start_block.astype(jnp.bfloat16)
    far = (fetch_whole(rounded),)
    back, kept = backward_loading(tiles[0, 0], offsets, place, rounded)
    first = apply(kept, far, give_back(*back))

    first_other = swap(first)
    far = tuple(decode(message) for message in fetch(first))
    first, first_other = decode(first), decode(first_other)
    back = backward_product(kept, offsets, place, first, first_other)
    second = apply(kept, far, give_back(*back))

    second_other = swap(second)
    second = decode(second)
    (found,) = small_call(
        gram_kernel,
        "gram",
        (jax.ShapeDtypeStruct((2 * rows, 8, columns), jnp.float32),),
        start_block.reshape(blocks, height // blocks, columns), first, second, first=place,
    )
    found = lax.all_to_all(found, ("row", "half"), 0, 0)
    found, second_other = lax.optimization_barrier((found, second_other))
    in_blocks = [
        value.reshape(-1, height // blocks, columns)
        for value in (start_block, first, first_other, second, decode(second_other))
    ]
    alphas, betas, q_third = small_call(
        functools.partial(last_kernel, height * rows),
        "last",
        (
            jax.ShapeDtypeStruct((2, columns), jnp.float32),
            jax.ShapeDtypeStruct((2, columns), jnp.float32),
            jax.ShapeDtypeStruct((blocks, height // blocks, columns), jnp.float32),
        ),
        found, *in_blocks, first=place,
    )
    return (alphas, betas, q_third.reshape(height, columns))


def solution(mesh):
    rows, cols = mesh.devices.shape
    parted = jax.sharding.Mesh(mesh.devices.reshape(rows, 2, cols // 2), AXES)
    split = ("half", "line")
    placed = (P("row", None), P("row", split, None, None, None, None), P("row", split, None))
    return jax.shard_map(
        body, mesh=parted, in_specs=placed, out_specs=(P(), P(), P("row", None)), check_vma=False
    )
```

```python
import functools

import jax
import jax.numpy as jnp
from jax import lax
from jax.experimental import pallas as pl
from jax.experimental.pallas import tpu as pltpu
from jax.sharding import PartitionSpec as P

EPS = 1e-06
TINY = 1e-30
WIRE = jnp.float16
SEGMENT_SCALE = 1024.0
CODE_ROWS = 8
ROWS_PER_STEP = 8
VMEM_LIMIT = 24 * 2**20
ROUND_VMEM_LIMIT = 61 * 2**20
ROUND_PARTS = 8
LOADING_VMEM_LIMIT = 53 * 2**20


def whole_vmem():
    return pl.BlockSpec(memory_space=pltpu.VMEM)


def whole_smem():
    return pl.BlockSpec(memory_space=pltpu.SMEM)


def low_part(value, high):
    return (value - high.astype(jnp.float32)).astype(jnp.bfloat16)


def code_of(squares, rows):
    return jnp.floor(jnp.log2(SEGMENT_SCALE * lax.rsqrt(squares * (1.0 / rows) + TINY)))


def merged(total, columns, axis):
    if total.shape[axis] == columns:
        return total
    return sum(jnp.split(total, 2, axis=axis))


def forward_rows(begin, offsets, tiles, halves, out, factor):
    blocks, width = halves.shape[:2]
    kept = tiles.shape[1]

    @pl.loop(0, blocks // 2 // ROWS_PER_STEP)
    def _(step):
        for local in range(ROWS_PER_STEP):
            at = step * ROWS_PER_STEP + local
            row = begin + at
            total = jnp.zeros((width, halves.shape[2]), jnp.float32)
            for k in range(0, kept, 2):
                first = halves[(row + offsets[k]) & (blocks - 1)]
                second = halves[(row + offsets[k + 1]) & (blocks - 1)]
                left = jnp.concatenate([tiles[row, k], tiles[row, k + 1]], axis=1)
                right = jnp.concatenate([first, second], axis=0)
                total += jnp.dot(left, right, preferred_element_type=jnp.float32)
            result = merged(total, out.shape[1], 1)
            out[pl.ds(pl.multiple_of(at * width, width), width)] = (
                result if factor is None else result * factor
            )


def forward_start_kernel(offsets, half, tiles, far, out):
    blocks, width, columns = far.shape
    squares = jnp.zeros((1, columns), jnp.float32)
    for block in range(blocks):
        value = far[block].astype(jnp.float32)
        squares += jnp.sum(value * value, axis=0, keepdims=True)
    code = code_of(squares, blocks * width)
    out[blocks // 2 * width :] = jnp.broadcast_to(code, (CODE_ROWS, columns))
    begin = (1 - half[0]) * (blocks // 2)
    forward_rows(begin, offsets, tiles, far, out, jnp.exp2(code))


def forward_first_kernel(offsets, half, tiles, own_half, other_half, out, halves):
    each, width, columns = own_half.shape
    start = half[0] * each
    squares = jnp.zeros((1, columns), jnp.float32)
    for block in range(each):
        for source, base in ((own_half, start), (other_half, each - start)):
            value = source[block]
            squares += jnp.sum(value * value, axis=0, keepdims=True)
            high = value.astype(jnp.bfloat16)
            halves[base + block] = jnp.concatenate([high, low_part(value, high)], axis=1)
    code = code_of(squares, 2 * each * width)
    out[each * width :] = jnp.broadcast_to(code, (CODE_ROWS, columns))
    forward_rows(each - start, offsets, tiles, halves, out, jnp.exp2(code))


def forward_second_kernel(offsets, half, tiles, halves, out):
    forward_rows(half[0] * (halves.shape[0] // 2), offsets, tiles, halves, out, None)


def turn_rows(block, value, squares, turned):
    squares[...] += jnp.sum(value * value, axis=0, keepdims=True)
    value = value.T
    high = value.astype(jnp.bfloat16)
    if turned.shape[1] == high.shape[0]:
        turned[block] = high
    else:
        turned[block] = jnp.concatenate([high, low_part(value, high)], axis=0)


def backward_block(block, kinds, offsets, tiles, turned):
    blocks, columns, width = turned.shape
    total = jnp.zeros((columns, width), jnp.float32)
    for k in kinds:
        first = (block + blocks - offsets[k]) & (blocks - 1)
        second = (block + blocks - offsets[k + 1]) & (blocks - 1)
        left = jnp.concatenate([turned[first], turned[second]], axis=1)
        right = jnp.concatenate([tiles[first, k], tiles[second, k + 1]], axis=0)
        total += jnp.dot(left, right, preferred_element_type=jnp.float32)
    return total


def backward_rows(start, kinds, offsets, tiles, squares, turned, given, out):
    blocks, _, width = turned.shape
    columns = squares.shape[1]
    each = blocks // 2
    code = code_of(squares[...], blocks * width)
    scale = jnp.exp2(code)
    for part in range(2):
        out[part, each * width :] = jnp.broadcast_to(code, (CODE_ROWS, columns))

        @pl.loop(0, each // ROWS_PER_STEP)
        def _(step):
            for local in range(ROWS_PER_STEP):
                at = step * ROWS_PER_STEP + local
                block = (start + part * each + at) & (blocks - 1)
                total = backward_block(block, kinds, offsets, tiles, turned)
                if given is not None:
                    total += given[block]
                result = merged(total, columns, 0).T * scale
                out[part, pl.ds(pl.multiple_of(at * width, width), width)] = result


def backward_loading_kernel(offsets, half, source, near, out, tiles, squares, turned, given, arrived):
    blocks = near.shape[0]
    steps = arrived.shape[0]
    each = tiles.shape[1] // steps

    def load(step):
        part = pl.ds(step * each, each)
        return pltpu.make_async_copy(source.at[:, part], tiles.at[:, part], arrived.at[step])

    for step in range(steps):
        load(step).start()
    squares[...] = jnp.zeros_like(squares)
    for block in range(blocks):
        turn_rows(block, near[block].astype(jnp.float32), squares, turned)
    for step in range(steps):
        load(step).wait()
        kinds = range(step * each, (step + 1) * each, 2)
        if step == steps - 1:
            backward_rows(
                half[0] * (blocks // 2), kinds, offsets, tiles, squares, turned, given, out
            )
            continue

        @pl.loop(0, blocks // ROWS_PER_STEP)
        def _(at):
            for local in range(ROWS_PER_STEP):
                block = at * ROWS_PER_STEP + local
                total = backward_block(block, kinds, offsets, tiles, turned)
                given[block] = total if step == 0 else given[block] + total


def backward_kernel(offsets, half, tiles, own_half, other_half, out, squares, turned):
    each = own_half.shape[0]
    start = half[0] * each
    squares[...] = jnp.zeros_like(squares)
    for block in range(each):
        turn_rows(start + block, own_half[block], squares, turned)
        turn_rows(each - start + block, other_half[block], squares, turned)
    kinds = range(0, tiles.shape[1], 2)
    backward_rows(start, kinds, offsets, tiles, squares, turned, None, out)


def round_kernel(source, out, value, arrived):
    parts = arrived.shape[0]
    rows = out.shape[0] // parts

    def load(part):
        at = pl.ds(part * rows, rows)
        return pltpu.make_async_copy(source.at[at], value.at[at], arrived.at[part])

    for part in range(parts):
        load(part).start()
    for part in range(parts):
        load(part).wait()
        at = pl.ds(part * rows, rows)
        out[at] = value[at].astype(out.dtype)


def rounded_block(value):
    return pl.pallas_call(
        round_kernel,
        out_shape=pltpu.VMEM(value.shape, jnp.bfloat16),
        in_specs=[pl.BlockSpec(memory_space=pl.ANY)],
        out_specs=whole_vmem(),
        scratch_shapes=[
            pltpu.VMEM(value.shape, value.dtype),
            pltpu.SemaphoreType.DMA((ROUND_PARTS,)),
        ],
        compiler_params=pltpu.CompilerParams(vmem_limit_bytes=ROUND_VMEM_LIMIT),
        cost_estimate=pl.CostEstimate(flops=0, bytes_accessed=2**16, transcendentals=0),
        name="round",
    )(value)


def gram_kernel(half, start, first, second, out):
    count, width, columns = first.shape
    begin = half[0] * count

    def total(function):
        sums = jnp.zeros((width, columns), jnp.float32)
        for block in range(count):
            sums += function(start[begin + block], first[block], second[block])
        return jnp.sum(sums, axis=0, keepdims=True)

    weight = total(lambda s, u, v: s * s)
    usable = weight > 0
    safe = jnp.where(usable, weight, 1.0)
    a = jnp.where(usable, total(lambda s, u, v: s * u) / safe, 0.0)
    b = jnp.where(usable, total(lambda s, u, v: s * (v - a * u)) / safe, 0.0)
    uu = total(lambda s, u, v: (u - a * s) * (u - a * s))
    uv = total(lambda s, u, v: (u - a * s) * (v - a * u - b * s))
    vv = total(lambda s, u, v: (v - a * u - b * s) * (v - a * u - b * s))
    values = jnp.concatenate([a, b, weight, uu, uv, vv, uu, uu], axis=0)
    for copy in range(out.shape[0]):
        out[copy] = values


def last_kernel(count, half, found, start, first_own, first_other, second_own, second_other, alphas, betas, out):
    a, b, weight, uu, uv, vv = (found[:, k, :] for k in range(6))

    def mean(value):
        return jnp.sum(value, axis=0, keepdims=True) * (1.0 / count)

    norm = jnp.sqrt(mean(weight) + EPS)
    inverse = 1.0 / norm
    alpha_one = mean(a * weight) * inverse * inverse
    delta = a - alpha_one
    beta_one = jnp.sqrt(mean(uu + delta * delta * weight) * inverse * inverse + EPS)
    k = inverse / beta_one
    shift = b + delta * a - beta_one * beta_one
    alpha_two = k * k * mean(uv + delta * uu + delta * shift * weight)
    along = delta - alpha_two
    rest = shift - alpha_two * delta
    square = mean(vv + 2.0 * along * uv + along * along * uu + rest * rest * weight)
    beta_two = jnp.sqrt(k * k * square + EPS)
    alphas[...] = jnp.concatenate([alpha_one, alpha_two], axis=0)
    betas[...] = jnp.concatenate([beta_one, beta_two], axis=0)
    of_start = (k * alpha_one * alpha_two - beta_one * inverse) / beta_two
    of_first = -k * (alpha_one + alpha_two) / beta_two
    of_second = k / beta_two
    each = first_own.shape[0]
    begin = half[0] * each
    for first, second, base in (
        (first_own, second_own, begin),
        (first_other, second_other, each - begin),
    ):
        for block in range(each):
            out[base + block] = (
                of_start * start[base + block] + of_first * first[block] + of_second * second[block]
            )


def small_call(kernel, name, out_shape, *values, first=None):
    specs = [whole_vmem()] * len(values)
    if first is not None:
        specs = [whole_smem()] + specs
        values = (first,) + values
    return pl.pallas_call(
        kernel,
        out_shape=out_shape,
        in_specs=specs,
        out_specs=tuple(whole_vmem() for _ in out_shape),
        compiler_params=pltpu.CompilerParams(vmem_limit_bytes=VMEM_LIMIT),
        cost_estimate=pl.CostEstimate(flops=0, bytes_accessed=2**16, transcendentals=0),
        name=name,
    )(*values)


def call(kernel, name, out_shape, scratch, offsets, half, tiles, *values):
    loading = kernel is backward_loading_kernel
    beside = kernel is forward_second_kernel
    return pl.pallas_call(
        kernel,
        out_shape=out_shape,
        in_specs=[whole_smem(), whole_smem(), pl.BlockSpec(memory_space=pl.ANY) if loading else whole_vmem()]
        + [whole_vmem()] * len(values),
        out_specs=tuple(whole_vmem() for _ in out_shape),
        scratch_shapes=scratch,
        compiler_params=pltpu.CompilerParams(
            vmem_limit_bytes=LOADING_VMEM_LIMIT if loading else VMEM_LIMIT
        ),
        cost_estimate=pl.CostEstimate(
            flops=2**30 if beside else 0,
            bytes_accessed=2**20 if beside else 2**16,
            transcendentals=0,
        ),
        name=name,
    )(offsets, half, tiles, *values)


def forward_product(tiles, offsets, half, far):
    blocks, _, width, _ = tiles.shape
    columns = far[0].shape[-1]
    each = blocks // 2
    message = jax.ShapeDtypeStruct((each * width + CODE_ROWS, columns), jnp.float32)
    part = jax.ShapeDtypeStruct((each * width, columns), jnp.float32)
    if len(far) == 1:
        halves = far[0].reshape(blocks, width, columns)
        (other,) = call(
            forward_start_kernel, "forward_start", (message,), [], offsets, half, tiles, halves
        )
    else:
        other, halves = call(
            forward_first_kernel,
            "forward_first",
            (message, pltpu.VMEM((blocks, width, 2 * columns), jnp.bfloat16)),
            [],
            offsets, half, tiles, *(value.reshape(each, width, columns) for value in far),
        )
    (own,) = call(forward_second_kernel, "forward_second", (part,), [], offsets, half, tiles, halves)
    return other, own


def messages_shape(blocks, width, columns):
    return (2, blocks // 2 * width + CODE_ROWS, columns)


def backward_scratch(blocks, width, columns, halves):
    return [
        pltpu.VMEM((1, columns), jnp.float32),
        pltpu.VMEM((blocks, halves * columns, width), jnp.bfloat16),
    ]


def backward_loading(tiles, offsets, half, near):
    blocks, _, width, _ = tiles.shape
    columns = near.shape[-1]
    out, kept = call(
        backward_loading_kernel,
        "backward_loading",
        (
            pltpu.VMEM(messages_shape(blocks, width, columns), jnp.float32),
            pltpu.VMEM(tiles.shape, tiles.dtype),
        ),
        backward_scratch(blocks, width, columns, 1)
        + [pltpu.VMEM((blocks, columns, width), jnp.float32), pltpu.SemaphoreType.DMA((3,))],
        offsets, half, tiles, near.reshape(blocks, width, columns),
    )
    return (out[0].astype(WIRE), out[1].astype(WIRE)), kept


def backward_product(tiles, offsets, half, own_half, other_half):
    blocks, _, width, _ = tiles.shape
    columns = own_half.shape[-1]
    shape = (blocks // 2, width, columns)
    (out,) = call(
        backward_kernel,
        "backward",
        (jax.ShapeDtypeStruct(messages_shape(blocks, width, columns), jnp.float32),),
        backward_scratch(blocks, width, columns, 2),
        offsets, half, tiles, own_half.reshape(shape), other_half.reshape(shape),
    )
    return out[0].astype(WIRE), out[1].astype(WIRE)


AXES = ("row", "half", "line")


def permute(value, place):
    rows = lax.axis_size("row")
    cols = lax.axis_size("half") * lax.axis_size("line")
    pairs = []
    for r in range(rows):
        for c in range(cols):
            to_row, to_col = place(r, c, c ^ (cols // 2))
            pairs.append((r * cols + c, to_row % rows * cols + to_col))
    return lax.ppermute(value, AXES, pairs)


def swap(value):
    return permute(value, lambda r, c, o: (r, o))


def fetch(value):
    own = permute(value, lambda r, c, o: (r - c, c))
    return own, permute(value, lambda r, c, o: (r - o, o))


def fetch_whole(value):
    return permute(value, lambda r, c, o: (r - o, o))


def give_back(own, other):
    same = permute(own, lambda r, c, o: (r + c, c))
    return same, permute(other, lambda r, c, o: (r + c, o))


def pack(value, code):
    codes = jnp.broadcast_to(code, value.shape[:-2] + (CODE_ROWS, value.shape[-1]))
    return jnp.concatenate([(value * jnp.exp2(code)).astype(WIRE), codes.astype(WIRE)], axis=-2)


def code_in(message):
    rows = message.shape[-2] - CODE_ROWS
    return message[..., rows : rows + 1, :].astype(jnp.float32)


def decode(message):
    rows = message.shape[-2] - CODE_ROWS
    return message[..., :rows, :].astype(jnp.float32) * jnp.exp2(-code_in(message))


def sum_line(partial, code):
    count = lax.axis_size("line")
    rows, columns = partial.shape
    parts = pack(partial.reshape(count, rows // count, columns), code)
    parts = lax.all_to_all(parts, "line", 0, 0)
    code = jnp.min(code_in(parts), axis=0) - (count - 1).bit_length()
    share = pack(jnp.sum(decode(parts), axis=0), code)
    return lax.all_to_all(jnp.broadcast_to(share[None], parts.shape), "line", 0, 0)


def body(start_block, tiles, band_offsets):
    half = lax.axis_index("half")
    rows, height, columns = lax.axis_size("row"), *start_block.shape
    parts = lax.axis_size("line")
    blocks = tiles.shape[2]
    offsets = band_offsets[0, 0]
    place = half[None].astype(jnp.int32)
    def apply(kept, far, back):
        other, own = forward_product(kept, offsets, place, far)
        given = swap(other.astype(WIRE))
        own, *back = lax.optimization_barrier((own, *back))
        arrived = own + decode(back[0]) + decode(back[1])
        code = jnp.minimum(code_in(other), code_in(given))
        code = jnp.minimum(code, jnp.minimum(code_in(back[0]), code_in(back[1]))) - 2.0
        return sum_line(arrived + decode(given), code)

    rounded = rounded_block(start_block)
    far = (fetch_whole(rounded),)
    back, kept = backward_loading(tiles[0, 0], offsets, place, rounded)
    first = apply(kept, far, give_back(*back))

    first_other = swap(first)
    far = tuple(decode(message) for message in fetch(first))
    first, first_other = decode(first), decode(first_other)
    back = backward_product(kept, offsets, place, first, first_other)
    second = apply(kept, far, give_back(*back))

    second_other = swap(second)
    second = decode(second)
    (found,) = small_call(
        gram_kernel,
        "gram",
        (jax.ShapeDtypeStruct((2 * rows, 8, columns), jnp.float32),),
        start_block.reshape(blocks, height // blocks, columns), first, second, first=place,
    )
    found = lax.all_to_all(found, ("row", "half"), 0, 0)
    found, second_other = lax.optimization_barrier((found, second_other))
    in_blocks = [
        value.reshape(-1, height // blocks, columns)
        for value in (start_block, first, first_other, second, decode(second_other))
    ]
    alphas, betas, q_third = small_call(
        functools.partial(last_kernel, height * rows),
        "last",
        (
            jax.ShapeDtypeStruct((2, columns), jnp.float32),
            jax.ShapeDtypeStruct((2, columns), jnp.float32),
            jax.ShapeDtypeStruct((blocks, height // blocks, columns), jnp.float32),
        ),
        found, *in_blocks, first=place,
    )
    return (alphas, betas, q_third.reshape(height, columns))


def solution(mesh):
    rows, cols = mesh.devices.shape
    parted = jax.sharding.Mesh(mesh.devices.reshape(rows, 2, cols // 2), AXES)
    split = ("half", "line")
    placed = (P("row", None), P("row", split, None, None, None, None), P("row", split, None))
    return jax.shard_map(
        body, mesh=parted, in_specs=placed, out_specs=(P(), P(), P("row", None)), check_vma=False
    )
```

```python
import functools

import jax
import jax.numpy as jnp
from jax import lax
from jax.experimental import pallas as pl
from jax.experimental.pallas import tpu as pltpu
from jax.sharding import PartitionSpec as P

EPS = 1e-06
TINY = 1e-30
WIRE = jnp.float16
SEGMENT_SCALE = 1024.0
CODE_ROWS = 8
ROWS_PER_STEP = 8
VMEM_LIMIT = 24 * 2**20
LOADING_VMEM_LIMIT = 53 * 2**20


def whole_vmem():
    return pl.BlockSpec(memory_space=pltpu.VMEM)


def whole_smem():
    return pl.BlockSpec(memory_space=pltpu.SMEM)


def low_part(value, high):
    return (value - high.astype(jnp.float32)).astype(jnp.bfloat16)


def code_of(squares, rows):
    return jnp.floor(jnp.log2(SEGMENT_SCALE * lax.rsqrt(squares * (1.0 / rows) + TINY)))


def merged(total, columns, axis):
    if total.shape[axis] == columns:
        return total
    return sum(jnp.split(total, 2, axis=axis))


def forward_rows(begin, offsets, tiles, halves, out, factor):
    blocks, width = halves.shape[:2]
    kept = tiles.shape[1]

    @pl.loop(0, blocks // 2 // ROWS_PER_STEP)
    def _(step):
        for local in range(ROWS_PER_STEP):
            at = step * ROWS_PER_STEP + local
            row = begin + at
            total = jnp.zeros((width, halves.shape[2]), jnp.float32)
            for k in range(0, kept, 2):
                first = halves[(row + offsets[k]) & (blocks - 1)]
                second = halves[(row + offsets[k + 1]) & (blocks - 1)]
                left = jnp.concatenate([tiles[row, k], tiles[row, k + 1]], axis=1)
                right = jnp.concatenate([first, second], axis=0)
                total += jnp.dot(left, right, preferred_element_type=jnp.float32)
            result = merged(total, out.shape[1], 1)
            out[pl.ds(pl.multiple_of(at * width, width), width)] = (
                result if factor is None else result * factor
            )


def forward_start_kernel(offsets, half, tiles, far, out):
    blocks, width, columns = far.shape
    squares = jnp.zeros((1, columns), jnp.float32)
    for block in range(blocks):
        value = far[block].astype(jnp.float32)
        squares += jnp.sum(value * value, axis=0, keepdims=True)
    code = code_of(squares, blocks * width)
    out[blocks // 2 * width :] = jnp.broadcast_to(code, (CODE_ROWS, columns))
    begin = (1 - half[0]) * (blocks // 2)
    forward_rows(begin, offsets, tiles, far, out, jnp.exp2(code))


def forward_first_kernel(offsets, half, tiles, low_rows, high_rows, out, halves):
    each, width, columns = low_rows.shape
    start = half[0] * each
    squares = jnp.zeros((1, columns), jnp.float32)
    for block in range(each):
        for source, base in ((low_rows, 0), (high_rows, each)):
            value = source[block]
            squares += jnp.sum(value * value, axis=0, keepdims=True)
            high = value.astype(jnp.bfloat16)
            halves[base + block] = jnp.concatenate([high, low_part(value, high)], axis=1)
    code = code_of(squares, 2 * each * width)
    out[each * width :] = jnp.broadcast_to(code, (CODE_ROWS, columns))
    forward_rows(each - start, offsets, tiles, halves, out, jnp.exp2(code))


def forward_second_kernel(offsets, half, tiles, halves, out):
    forward_rows(half[0] * (halves.shape[0] // 2), offsets, tiles, halves, out, None)


def turn_rows(block, value, squares, turned):
    squares[...] += jnp.sum(value * value, axis=0, keepdims=True)
    value = value.T
    high = value.astype(jnp.bfloat16)
    if turned.shape[1] == high.shape[0]:
        turned[block] = high
    else:
        turned[block] = jnp.concatenate([high, low_part(value, high)], axis=0)


def backward_block(block, kinds, offsets, tiles, turned):
    blocks, columns, width = turned.shape
    total = jnp.zeros((columns, width), jnp.float32)
    for k in kinds:
        first = (block + blocks - offsets[k]) & (blocks - 1)
        second = (block + blocks - offsets[k + 1]) & (blocks - 1)
        left = jnp.concatenate([turned[first], turned[second]], axis=1)
        right = jnp.concatenate([tiles[first, k], tiles[second, k + 1]], axis=0)
        total += jnp.dot(left, right, preferred_element_type=jnp.float32)
    return total


def backward_rows(start, kinds, offsets, tiles, squares, turned, given, out):
    blocks, _, width = turned.shape
    columns = squares.shape[1]
    each = blocks // 2
    code = code_of(squares[...], blocks * width)
    scale = jnp.exp2(code)
    for part in range(2):
        out[part, each * width :] = jnp.broadcast_to(code, (CODE_ROWS, columns))

        @pl.loop(0, each // ROWS_PER_STEP)
        def _(step):
            for local in range(ROWS_PER_STEP):
                at = step * ROWS_PER_STEP + local
                block = (start + part * each + at) & (blocks - 1)
                total = backward_block(block, kinds, offsets, tiles, turned)
                if given is not None:
                    total += given[block]
                result = merged(total, columns, 0).T * scale
                out[part, pl.ds(pl.multiple_of(at * width, width), width)] = result


def backward_loading_kernel(offsets, half, source, near, out, tiles, squares, turned, given, arrived):
    blocks = near.shape[0]
    steps = arrived.shape[0]
    each = tiles.shape[1] // steps

    def load(step):
        part = pl.ds(step * each, each)
        return pltpu.make_async_copy(source.at[:, part], tiles.at[:, part], arrived.at[step])

    for step in range(steps):
        load(step).start()
    squares[...] = jnp.zeros_like(squares)
    for block in range(blocks):
        turn_rows(block, near[block].astype(jnp.float32), squares, turned)
    for step in range(steps):
        load(step).wait()
        kinds = range(step * each, (step + 1) * each, 2)
        if step == steps - 1:
            backward_rows(
                half[0] * (blocks // 2), kinds, offsets, tiles, squares, turned, given, out
            )
            continue

        @pl.loop(0, blocks // ROWS_PER_STEP)
        def _(at):
            for local in range(ROWS_PER_STEP):
                block = at * ROWS_PER_STEP + local
                total = backward_block(block, kinds, offsets, tiles, turned)
                given[block] = total if step == 0 else given[block] + total


def backward_kernel(offsets, half, tiles, near, out, squares, turned):
    blocks = near.shape[0]
    squares[...] = jnp.zeros_like(squares)
    for block in range(blocks):
        turn_rows(block, near[block], squares, turned)
    kinds = range(0, tiles.shape[1], 2)
    backward_rows(half[0] * (blocks // 2), kinds, offsets, tiles, squares, turned, None, out)


def gram_kernel(half, start, first, second, out):
    count, width, columns = second.shape
    begin = half[0] * count

    def total(function):
        sums = jnp.zeros((width, columns), jnp.float32)
        for block in range(count):
            sums += function(start[begin + block], first[begin + block], second[block])
        return jnp.sum(sums, axis=0, keepdims=True)

    weight = total(lambda s, u, v: s * s)
    usable = weight > 0
    safe = jnp.where(usable, weight, 1.0)
    a = jnp.where(usable, total(lambda s, u, v: s * u) / safe, 0.0)
    b = jnp.where(usable, total(lambda s, u, v: s * (v - a * u)) / safe, 0.0)
    uu = total(lambda s, u, v: (u - a * s) * (u - a * s))
    uv = total(lambda s, u, v: (u - a * s) * (v - a * u - b * s))
    vv = total(lambda s, u, v: (v - a * u - b * s) * (v - a * u - b * s))
    values = jnp.concatenate([a, b, weight, uu, uv, vv, uu, uu], axis=0)
    for copy in range(out.shape[0]):
        out[copy] = values


def last_kernel(count, half, found, start, first, second_own, second_other, alphas, betas, out):
    a, b, weight, uu, uv, vv = (found[:, k, :] for k in range(6))

    def mean(value):
        return jnp.sum(value, axis=0, keepdims=True) * (1.0 / count)

    norm = jnp.sqrt(mean(weight) + EPS)
    inverse = 1.0 / norm
    alpha_one = mean(a * weight) * inverse * inverse
    delta = a - alpha_one
    beta_one = jnp.sqrt(mean(uu + delta * delta * weight) * inverse * inverse + EPS)
    k = inverse / beta_one
    shift = b + delta * a - beta_one * beta_one
    alpha_two = k * k * mean(uv + delta * uu + delta * shift * weight)
    along = delta - alpha_two
    rest = shift - alpha_two * delta
    square = mean(vv + 2.0 * along * uv + along * along * uu + rest * rest * weight)
    beta_two = jnp.sqrt(k * k * square + EPS)
    alphas[...] = jnp.concatenate([alpha_one, alpha_two], axis=0)
    betas[...] = jnp.concatenate([beta_one, beta_two], axis=0)
    of_start = (k * alpha_one * alpha_two - beta_one * inverse) / beta_two
    of_first = -k * (alpha_one + alpha_two) / beta_two
    of_second = k / beta_two
    each = second_own.shape[0]
    begin = half[0] * each
    for second, base in ((second_own, begin), (second_other, each - begin)):
        for block in range(each):
            at = base + block
            out[at] = of_start * start[at] + of_first * first[at] + of_second * second[block]


def small_call(kernel, name, out_shape, *values, first=None):
    specs = [whole_vmem()] * len(values)
    if first is not None:
        specs = [whole_smem()] + specs
        values = (first,) + values
    return pl.pallas_call(
        kernel,
        out_shape=out_shape,
        in_specs=specs,
        out_specs=tuple(whole_vmem() for _ in out_shape),
        compiler_params=pltpu.CompilerParams(vmem_limit_bytes=VMEM_LIMIT),
        cost_estimate=pl.CostEstimate(flops=0, bytes_accessed=2**16, transcendentals=0),
        name=name,
    )(*values)


def call(kernel, name, out_shape, scratch, offsets, half, tiles, *values):
    loading = kernel is backward_loading_kernel
    beside = kernel is forward_second_kernel
    return pl.pallas_call(
        kernel,
        out_shape=out_shape,
        in_specs=[whole_smem(), whole_smem(), pl.BlockSpec(memory_space=pl.ANY) if loading else whole_vmem()]
        + [whole_vmem()] * len(values),
        out_specs=tuple(whole_vmem() for _ in out_shape),
        scratch_shapes=scratch,
        compiler_params=pltpu.CompilerParams(
            vmem_limit_bytes=LOADING_VMEM_LIMIT if loading else VMEM_LIMIT
        ),
        cost_estimate=pl.CostEstimate(
            flops=2**30 if beside else 0,
            bytes_accessed=2**20 if beside else 2**16,
            transcendentals=0,
        ),
        name=name,
    )(offsets, half, tiles, *values)


def forward_product(tiles, offsets, half, far):
    blocks, _, width, _ = tiles.shape
    columns = far[0].shape[-1]
    each = blocks // 2
    message = jax.ShapeDtypeStruct((each * width + CODE_ROWS, columns), jnp.float32)
    part = jax.ShapeDtypeStruct((each * width, columns), jnp.float32)
    if len(far) == 1:
        halves = far[0].reshape(blocks, width, columns)
        (other,) = call(
            forward_start_kernel, "forward_start", (message,), [], offsets, half, tiles, halves
        )
    else:
        other, halves = call(
            forward_first_kernel,
            "forward_first",
            (message, pltpu.VMEM((blocks, width, 2 * columns), jnp.bfloat16)),
            [],
            offsets, half, tiles, *(value.reshape(each, width, columns) for value in far),
        )
    (own,) = call(forward_second_kernel, "forward_second", (part,), [], offsets, half, tiles, halves)
    return other, own


def messages_shape(blocks, width, columns):
    return (2, blocks // 2 * width + CODE_ROWS, columns)


def backward_scratch(blocks, width, columns, halves):
    return [
        pltpu.VMEM((1, columns), jnp.float32),
        pltpu.VMEM((blocks, halves * columns, width), jnp.bfloat16),
    ]


def backward_loading(tiles, offsets, half, near):
    blocks, _, width, _ = tiles.shape
    columns = near.shape[-1]
    out, kept = call(
        backward_loading_kernel,
        "backward_loading",
        (
            pltpu.VMEM(messages_shape(blocks, width, columns), jnp.float32),
            pltpu.VMEM(tiles.shape, tiles.dtype),
        ),
        backward_scratch(blocks, width, columns, 1)
        + [pltpu.VMEM((blocks, columns, width), jnp.float32), pltpu.SemaphoreType.DMA((3,))],
        offsets, half, tiles, near.reshape(blocks, width, columns),
    )
    return (out[0].astype(WIRE), out[1].astype(WIRE)), kept


def backward_product(tiles, offsets, half, near):
    blocks, _, width, _ = tiles.shape
    columns = near.shape[-1]
    (out,) = call(
        backward_kernel,
        "backward",
        (jax.ShapeDtypeStruct(messages_shape(blocks, width, columns), jnp.float32),),
        backward_scratch(blocks, width, columns, 2),
        offsets, half, tiles, near.reshape(blocks, width, columns),
    )
    return out[0].astype(WIRE), out[1].astype(WIRE)


AXES = ("row", "half", "line")


def permute(value, place):
    rows = lax.axis_size("row")
    cols = lax.axis_size("half") * lax.axis_size("line")
    pairs = []
    for r in range(rows):
        for c in range(cols):
            to_row, to_col = place(r, c, c ^ (cols // 2))
            pairs.append((r * cols + c, to_row % rows * cols + to_col))
    return lax.ppermute(value, AXES, pairs)


def swap(value):
    return permute(value, lambda r, c, o: (r, o))


def fetch(value):
    own = permute(value, lambda r, c, o: (r - c, c))
    return own, permute(value, lambda r, c, o: (r - o, o))


def fetch_whole(value):
    return permute(value, lambda r, c, o: (r - o, o))


def give_back(own, other):
    same = permute(own, lambda r, c, o: (r + c, c))
    return same, permute(other, lambda r, c, o: (r + c, o))


def pack(value, code):
    codes = jnp.broadcast_to(code, value.shape[:-2] + (CODE_ROWS, value.shape[-1]))
    return jnp.concatenate([(value * jnp.exp2(code)).astype(WIRE), codes.astype(WIRE)], axis=-2)


def code_in(message):
    rows = message.shape[-2] - CODE_ROWS
    return message[..., rows : rows + 1, :].astype(jnp.float32)


def decode(message):
    rows = message.shape[-2] - CODE_ROWS
    return message[..., :rows, :].astype(jnp.float32) * jnp.exp2(-code_in(message))


def sum_line(partial, code):
    count = lax.axis_size("line")
    rows, columns = partial.shape
    parts = pack(partial.reshape(count, rows // count, columns), code)
    parts = lax.all_to_all(parts, "line", 0, 0)
    code = jnp.min(code_in(parts), axis=0) - (count - 1).bit_length()
    return pack(jnp.sum(decode(parts), axis=0), code)


def gather(share, axes):
    copies = jnp.broadcast_to(share[None], (lax.axis_size(axes),) + share.shape)
    return lax.all_to_all(copies, axes, 0, 0)


def body(start_block, tiles, band_offsets):
    half = lax.axis_index("half")
    rows, height, columns = lax.axis_size("row"), *start_block.shape
    parts = lax.axis_size("line")
    blocks = tiles.shape[2]
    offsets = band_offsets[0, 0]
    place = half[None].astype(jnp.int32)
    def apply(kept, far, back):
        other, own = forward_product(kept, offsets, place, far)
        given = swap(other.astype(WIRE))
        own, *back = lax.optimization_barrier((own, *back))
        arrived = own + decode(back[0]) + decode(back[1])
        code = jnp.minimum(code_in(other), code_in(given))
        code = jnp.minimum(code, jnp.minimum(code_in(back[0]), code_in(back[1]))) - 2.0
        return sum_line(arrived + decode(given), code)

    rounded = start_block.astype(jnp.bfloat16)
    far = (fetch_whole(rounded),)
    back, kept = backward_loading(tiles[0, 0], offsets, place, rounded)
    first = gather(apply(kept, far, give_back(*back)), ("half", "line"))

    far = fetch_whole(first)
    far = (decode(far[:parts]), decode(far[parts:]))
    first = decode(first)
    back = backward_product(kept, offsets, place, first)
    second = gather(apply(kept, far, give_back(*back)), "line")

    second_other = swap(second)
    second = decode(second)
    (found,) = small_call(
        gram_kernel,
        "gram",
        (jax.ShapeDtypeStruct((2 * rows, 8, columns), jnp.float32),),
        start_block.reshape(blocks, height // blocks, columns), first, second, first=place,
    )
    found = lax.all_to_all(found, ("row", "half"), 0, 0)
    found, second_other = lax.optimization_barrier((found, second_other))
    in_blocks = [
        value.reshape(-1, height // blocks, columns)
        for value in (start_block, first, second, decode(second_other))
    ]
    alphas, betas, q_third = small_call(
        functools.partial(last_kernel, height * rows),
        "last",
        (
            jax.ShapeDtypeStruct((2, columns), jnp.float32),
            jax.ShapeDtypeStruct((2, columns), jnp.float32),
            jax.ShapeDtypeStruct((blocks, height // blocks, columns), jnp.float32),
        ),
        found, *in_blocks, first=place,
    )
    return (alphas, betas, q_third.reshape(height, columns))


def solution(mesh):
    rows, cols = mesh.devices.shape
    parted = jax.sharding.Mesh(mesh.devices.reshape(rows, 2, cols // 2), AXES)
    split = ("half", "line")
    placed = (P("row", None), P("row", split, None, None, None, None), P("row", split, None))
    return jax.shard_map(
        body, mesh=parted, in_specs=placed, out_specs=(P(), P(), P("row", None)), check_vma=False
    )
```
